128 devices in a mesh: grp: 8 (over x, core), dev: 16 (over z, y).
Axes of the slice: x: 4, y: 4, z: 4, core: 2. Of those that a mesh axis runs over, the one named last changes fastest.
Arguments:
- charges: bfloat16 [4096, 8, 256], P(('grp', 'dev')), may hold values from -6 to 6
- near_list: int32 [4096, 4], P(('grp', 'dev')), may hold values from 0 to 4095, as said below
- near_blocks: bfloat16 [4096, 4, 256, 256], P(('grp', 'dev')), may hold values from -0.1875 to 0.1875
- source_basis: bfloat16 [4096, 64, 256], P(('grp', 'dev')), may hold values from -0.375 to 0.375
- target_basis: bfloat16 [4096, 64, 256], P(('grp', 'dev')), may hold values from -0.75 to 0.75
- far_devices: int32 [4096, 8], P(('grp', 'dev')), may hold values from 0 to 127, all different within a row; in each aligned block of 32 rows (0 to 31, 32 to 63, ...) at most 4 rows name the same one
- far_slots: int32 [4096, 8], P(('grp', 'dev')), may hold values from 0 to 31
- far_couplings: bfloat16 [4096, 8, 64, 64], P(('grp', 'dev')), may hold values from -0.25 to 0.25
- up_transfer: bfloat16 [4096, 64, 64], P(('grp', 'dev')), may hold values from -0.125 to 0.125
- coarse_list: int32 [128, 6], P(('grp', 'dev')), may hold values from 0 to 127, as said below
- coarse_couplings: bfloat16 [128, 6, 64, 64], P(('grp', 'dev')), may hold values from -0.3125 to 0.3125
- down_transfer: bfloat16 [4096, 64, 64], P(('grp', 'dev')), may hold values from -0.75 to 0.75
Outputs:
- potentials: float32 [4096, 8, 256], P(('grp', 'dev'))
The draws below stay inside these ranges and needn't reach their ends.
Inputs may be any that keep to these rules, and one draw needn't show every extreme that they name: `near_list`: entry 0 of leaf l is l itself, entry 1 is max(l - 32, 0), entry 2 is min(l + 32, 4095); every entry of leaf l lies within 32 leaves of l. `far_devices`: each row names 8 different devices; in the rows of one device (aligned blocks of 32 rows) no device is named more than 4 times. `coarse_list`: row n names 6 different nodes, none of them n, all of the same subtree as n: nodes m with m // 16 == n // 16.
All inputs are finite; a program needn't handle non-finite values.
Results may differ from the reference program's by a relative error of at most 0.0045.
Values may be sent and summed in bfloat16 or wider, within the bound.
No kernel may reach another device: no remote copies, remote signals or barrier semaphores. Data moves between devices by JAX's collectives and lax.ppermute only.
A program may use at most 128 MiB of HBM per device.

```python
import math
import jax
import jax.numpy as jnp
import numpy as np
from jax import lax

LEAF = 256
K = 64
R = 8
LEAVES_DEV = 32
NNEAR = 4
NFAR = 8
NCOARSE = 6
LEAVES = 4096
NODES = 128
CAP = 4
N_DEV = 16
DEVICES = 128


def draw_near_list(key, part):
    key = jax.random.fold_in(key, 11)
    offsets = jax.random.randint(key, (LEAVES, NNEAR), -LEAVES_DEV, LEAVES_DEV + 1, dtype=jnp.int32)
    offsets = offsets.at[:, 0].set(0)
    offsets = offsets.at[:, 1].set(-LEAVES_DEV)
    offsets = offsets.at[:, 2].set(LEAVES_DEV)
    base = jnp.arange(LEAVES, dtype=jnp.int32)[:, None]
    return jnp.clip(base + offsets, 0, LEAVES - 1).astype(jnp.int32)


def draw_coarse_list(key, part):
    key = jax.random.fold_in(key, 23)
    keys = jax.random.split(key, NODES)
    others = jax.vmap(lambda single: jax.random.permutation(single, N_DEV - 2)[:NCOARSE - 1])(keys)
    steps = jnp.concatenate([jnp.ones((NODES, 1), jnp.int32), others.astype(jnp.int32) + 2], axis=1)
    nodes = jnp.arange(NODES, dtype=jnp.int32)
    start = nodes // N_DEV * N_DEV
    inner = nodes % N_DEV
    return (start[:, None] + (inner[:, None] + steps) % N_DEV).astype(jnp.int32)


def touch_ends(array, rng, low, top_value):
    longest = array.shape.index(max(array.shape))
    spots = []
    for shift in (0, 1):
        where = [jax.random.randint(jax.random.fold_in(rng, axis), (), 0, length) for axis, length in enumerate(array.shape)]
        where[longest] = (where[longest] + shift) % array.shape[longest]
        spots.append(tuple(where))
    return array.at[spots[0]].set(low).at[spots[1]].set(top_value)


def levels(stream_key, extent, cuts, smallest, high):
    loudness, own = 1.0, jax.random.fold_in(stream_key, 6)
    for axis_at, shards_of in cuts:
        heights = jnp.exp(jax.random.uniform(jax.random.fold_in(own, axis_at), (shards_of,), jnp.float32, smallest / len(cuts), high / len(cuts)))
        loudness = loudness * jnp.repeat(heights, extent[axis_at] // shards_of).reshape([-1 if axis == axis_at else 1 for axis in range(len(extent))])
    return loudness


def deal_out(own_key, own, number, rows, count, top, bound, lean):
    ranking = jax.random.permutation(own_key, count)
    packed, ordinary = shares(count, rows * top, bound, lean, True), shares(count, rows * top, bound, lean, False)
    places = jnp.arange(count)

    def named(lengths, turn):
        used = int((lengths > 0).sum())
        fixed = max(1, used // 4)
        passed = fixed + (places - fixed + turn * (used - fixed)) % max(1, count - fixed)
        return jnp.zeros((count,), jnp.int32).at[ranking[jnp.where(places < fixed, places, passed)]].set(jnp.asarray(lengths, jnp.int32))

    lengths = jnp.where(number % 4 == 0, named(packed, number // 4), named(ordinary, number - number // 4 - 1))
    mixed = jax.random.permutation(jax.random.fold_in(own, 3), count)
    giver, receiver = mixed[0:count // 2 * 2:2], mixed[1:count // 2 * 2:2]
    room = jnp.minimum(lengths[giver] - 1, bound - lengths[receiver]) // 2
    room = jnp.where((giver == ranking[0]) | (receiver == ranking[0]) | (lengths[receiver] == 0), 0, jnp.maximum(room, 0))
    passed = jax.random.randint(jax.random.fold_in(own, 4), (count // 2,), 0, 1 << 20) % (room + 1)
    lengths = lengths.at[giver].add(-passed).at[receiver].add(passed)
    labels = jnp.searchsorted(jnp.cumsum(lengths), jnp.arange(rows * top), side="right").astype(jnp.int32)
    listing = labels.reshape(top, rows).T
    listing = listing[jax.random.permutation(jax.random.fold_in(own, 1), rows)]
    turn = jax.random.randint(jax.random.fold_in(own, 2), (rows, 1), 0, top)
    return jnp.take_along_axis(listing, (jnp.arange(top)[None, :] + turn) % top, axis=1)


def shares(number_of, total, bound, skew, full):
    weights = [(1 << 20) // math.isqrt(standing ** skew) + 1 for standing in range(1, number_of + 1)]
    largest = bound if full else min(bound, max(-(-total // number_of), total * weights[0] // sum(weights)))
    least = 1 if total - largest >= number_of - 1 else 0
    counts, surplus = [largest] + [least] * (number_of - 1), total - largest - least * (number_of - 1)
    while surplus > 0:
        movable = [i for i in range(1, number_of) if counts[i] < largest] or [i for i in range(1, number_of) if counts[i] < bound]
        whole, remaining = sum([weights[i] for i in movable]), surplus
        for i in movable:
            extra = min(bound - counts[i], max(1, remaining * weights[i] // whole), surplus)
            counts[i] = counts[i] + extra
            surplus = surplus - extra
    return np.array(counts)


def centred(stream_key, extent, deviation, limit, pieces=(), kind=jnp.bfloat16):
    values = jax.random.normal(stream_key, extent, jnp.float32) * deviation
    if len(pieces) > 0:
        values = levels(stream_key, extent, pieces, -0.22, 0.18) * values
    return jnp.clip(values, min=-limit, max=limit).astype(kind)


def setup_inputs(seed: int = 0) -> dict:
    streams_of = jax.random.split(jax.random.key(seed), 13)
    charges = centred(streams_of[0], (LEAVES, R, LEAF), 1.0, 6.0, ((0, 128),))
    near_list = draw_near_list(jax.random.fold_in(streams_of[12], 71), 0)
    near_blocks = centred(streams_of[2], (LEAVES, NNEAR, LEAF, LEAF), (LEAF * NNEAR) ** -0.5, 0.1875, ((0, 128),))
    source_basis = centred(streams_of[3], (LEAVES, K, LEAF), LEAF ** -0.5, 0.375, ((0, 128),))
    target_basis = centred(streams_of[4], (LEAVES, K, LEAF), K ** -0.5, 0.75, ((0, 128),))
    far_devices_keys = jax.random.split(jax.random.fold_in(streams_of[5], 1), LEAVES // LEAVES_DEV)
    far_devices_turns = jax.random.permutation(jax.random.fold_in(streams_of[5], 3), LEAVES // LEAVES_DEV)
    far_devices = jax.vmap(lambda own, number: deal_out(jax.random.fold_in(streams_of[5], 2), own, number, LEAVES_DEV, DEVICES, NFAR, CAP, 2))(far_devices_keys, far_devices_turns).reshape((LEAVES, NFAR))
    far_slots = touch_ends(jax.random.randint(streams_of[6], (LEAVES, NFAR), 0, LEAVES_DEV), jax.random.fold_in(streams_of[6], 1), 0, LEAVES_DEV - 1).astype(jnp.int32)
    far_couplings = centred(streams_of[7], (LEAVES, NFAR, K, K), (K * NFAR) ** -0.5, 0.25, ((0, 128),))
    up_transfer = centred(streams_of[8], (LEAVES, K, K), (K * LEAVES_DEV) ** -0.5, 0.125, ((0, 128),))
    coarse_list = draw_coarse_list(jax.random.fold_in(streams_of[12], 71), 0)
    coarse_couplings = centred(streams_of[10], (NODES, NCOARSE, K, K), (K * NCOARSE) ** -0.5, 0.3125, ((0, 128),))
    down_transfer = centred(streams_of[11], (LEAVES, K, K), K ** -0.5, 0.75, ((0, 128),))
    return {"charges": charges, "near_list": near_list, "near_blocks": near_blocks, "source_basis": source_basis, "target_basis": target_basis, "far_devices": far_devices, "far_slots": far_slots, "far_couplings": far_couplings, "up_transfer": up_transfer, "coarse_list": coarse_list, "coarse_couplings": coarse_couplings, "down_transfer": down_transfer}


def reference(charges, near_list, near_blocks, source_basis, target_basis, far_devices, far_slots, far_couplings, up_transfer, coarse_list, coarse_couplings, down_transfer):
    widened = charges.astype(jnp.float32)
    moments = jnp.einsum("lkp,lrp->lrk", source_basis.astype(jnp.float32), widened).astype(jnp.bfloat16)

    def near_leaf(item):
        near_rows, blocks = item
        picked = jnp.take(widened, near_rows, axis=0)
        return jnp.einsum("jpq,jrq->rp", blocks.astype(jnp.float32), picked)

    near_field = lax.map(near_leaf, (near_list, near_blocks))

    def far_leaf(item):
        couplings, moment = item
        return jnp.einsum("jkq,rq->jrk", couplings.astype(jnp.float32), moment.astype(jnp.float32))

    products = lax.map(far_leaf, (far_couplings, moments))
    targets = (far_devices * LEAVES_DEV + far_slots).reshape(-1).astype(jnp.int32)
    far_sum = jnp.zeros((LEAVES, R, K), jnp.float32).at[targets].add(products.reshape(LEAVES * NFAR, R, K))

    grouped = moments.astype(jnp.float32).reshape(NODES, LEAVES_DEV, R, K)
    upward = up_transfer.astype(jnp.float32).reshape(NODES, LEAVES_DEV, K, K)
    node_moment = jnp.einsum("nlkq,nlrq->nrk", upward, grouped).astype(jnp.bfloat16)
    picked_nodes = jnp.take(node_moment, coarse_list, axis=0).astype(jnp.float32)
    coarse_local = jnp.einsum("njkq,njrq->nrk", coarse_couplings.astype(jnp.float32), picked_nodes).astype(jnp.bfloat16)
    downward = down_transfer.astype(jnp.float32).reshape(NODES, LEAVES_DEV, K, K)
    descended = jnp.einsum("nlkq,nrq->nlrk", downward, coarse_local.astype(jnp.float32)).reshape(LEAVES, R, K)
    local_field = (far_sum + descended).astype(jnp.bfloat16)
    return near_field + jnp.einsum("lkp,lrk->lrp", target_basis.astype(jnp.float32), local_field.astype(jnp.float32))
```

```python
import jax
import jax.numpy as jnp
from jax import lax
from jax.experimental import pallas as pl
from jax.experimental.pallas import tpu as pltpu
from jax.sharding import PartitionSpec as P

AXES = ("grp", "dev")
LEAVES = 32
RHS = 8
RANK = 64
POINTS = 256
NFAR = 8
NNEAR = 4
NCOARSE = 6
DEVICES = 128
BF16 = jnp.bfloat16
F32 = jnp.float32
NT = (((1,), (1,)), ((), ()))
TN = (((0,), (0,)), ((), ()))
MIB = 1 << 20


def dot(a, b, dims=(((1,), (0,)), ((), ()))):
    return lax.dot_general(a, b, dims, preferred_element_type=F32)


def iota(shape, dim):
    return lax.broadcasted_iota(jnp.int32, shape, dim)


GROUP = 4


def in_hbm(*arrays):
    return tuple(pltpu.with_memory_space_constraint(array, pltpu.HBM) for array in arrays)


def outgoing_kernel(
    charges,
    devices,
    slots,
    basis,
    couplings,
    transfer,
    send,
    charges_v,
    devices_v,
    slots_v,
    basis_v,
    couplings_v,
    transfer_v,
    products,
    sems,
):
    steps = LEAVES // GROUP
    small = [
        pltpu.make_async_copy(src, dst, sems.at[3, i])
        for i, (src, dst) in enumerate(((charges, charges_v), (devices, devices_v), (slots, slots_v)))
    ]
    for copy in small:
        copy.start()
    copies = []
    for g in range(steps):
        part = pl.ds(g * GROUP, GROUP)
        copies.append(
            [
                pltpu.make_async_copy(src.at[part], dst.at[part], sems.at[i, g])
                for i, (src, dst) in enumerate(
                    ((basis, basis_v), (couplings, couplings_v), (transfer, transfer_v))
                )
            ]
        )
        for copy in copies[-1]:
            copy.start()
    for copy in small:
        copy.wait()

    entries = LEAVES * NFAR
    device = jnp.concatenate([devices_v[j : j + 1, :] for j in range(NFAR)], axis=1)
    slot = jnp.concatenate([slots_v[j : j + 1, :] for j in range(NFAR)], axis=1)
    named = iota((DEVICES, entries), 0) == device
    earlier = iota((entries, entries), 0) < iota((entries, entries), 1)
    counts = dot(named.astype(BF16), earlier.astype(BF16))
    order = jnp.sum(jnp.where(named, counts, 0.0), axis=0, keepdims=True).astype(jnp.int32)
    row_of = device * 8 + order
    slot_rows = jnp.broadcast_to((slot + 1).astype(F32), (128, entries)).astype(BF16)

    node = jnp.zeros((RHS, RANK), F32)
    for g in range(steps):
        for copy in copies[g]:
            copy.wait()
        at = g * GROUP
        rows = GROUP * RHS
        own = charges_v[at : at + GROUP].reshape(rows, POINTS)
        all_moments = dot(own, basis_v[at : at + GROUP].reshape(GROUP * RANK, POINTS), NT)
        moments = [
            all_moments[i * RHS : (i + 1) * RHS, i * RANK : (i + 1) * RANK].astype(BF16)
            for i in range(GROUP)
        ]
        raised = dot(
            jnp.concatenate(moments, axis=0), transfer_v[at : at + GROUP].reshape(GROUP * RANK, RANK), NT
        )
        for i in range(GROUP):
            node += raised[i * RHS : (i + 1) * RHS, i * RANK : (i + 1) * RANK]
            for h in range(2):
                half = couplings_v[at + i, h * 4 : h * 4 + 4].reshape(4 * RANK, RANK)
                product = dot(moments[i], half, NT)
                for t in range(2):
                    products[2 * h + t, (at + i) * RHS : (at + i + 1) * RHS, :] = product[
                        :, t * 128 : (t + 1) * 128
                    ]

    low = iota((LEAVES, 128), 1) < RANK
    pieces = []
    for c in range(4):
        piece = []
        for t in range(NFAR // 2):
            first = products[t, pl.ds(c, LEAVES, stride=RHS), :]
            second = products[t, pl.ds(c + 4, LEAVES, stride=RHS), :]
            piece.append(jnp.where(low, first, pltpu.roll(second, RANK, 1)))
            piece.append(jnp.where(low, pltpu.roll(first, RANK, 1), second))
        pieces.append(jnp.concatenate(piece, axis=0).astype(BF16))
    table = jnp.concatenate(
        [
            jnp.concatenate([pieces[0], pieces[2]], axis=1),
            jnp.concatenate([pieces[1], pieces[3]], axis=1),
        ],
        axis=0,
    )
    wide = jnp.concatenate([node, jnp.zeros((RHS, RANK), F32)], axis=1)
    turned = pltpu.roll(pltpu.roll(wide, RANK, 1), 4, 0)
    upper = iota((RHS, 128), 0) < 4
    node_rows = jnp.where(upper, jnp.where(iota((RHS, 128), 1) < RANK, wide, turned), 0.0)

    span = 256
    for at in range(0, DEVICES * 8, span):
        row = iota((span, entries), 0) + at
        chosen = (row == row_of).astype(BF16)
        second = (row == row_of + 4).astype(BF16)
        rows = dot(jnp.concatenate([chosen, second], axis=1), table)
        names = dot(second, slot_rows, NT).reshape(span // 8, 8, 128) + node_rows[None]
        part = pl.ds(at // 8, span // 8)
        send[part, 0] = rows[:, :128].reshape(span // 8, 8, 128).astype(BF16)
        send[part, 1] = rows[:, 128:].reshape(span // 8, 8, 128).astype(BF16)
        send[part, 2] = names.astype(BF16)


def outgoing(charges, far_devices, far_slots, source_basis, far_couplings, up_transfer):
    arrays = (charges, far_devices.T, far_slots.T, source_basis, far_couplings, up_transfer)
    return pl.pallas_call(
        outgoing_kernel,
        out_shape=jax.ShapeDtypeStruct((DEVICES, 3, 8, 128), BF16),
        in_specs=[pl.BlockSpec(memory_space=pltpu.HBM)] * 6,
        out_specs=pl.BlockSpec(memory_space=pltpu.VMEM),
        scratch_shapes=[pltpu.VMEM(array.shape, array.dtype) for array in arrays]
        + [
            pltpu.VMEM((NFAR // 2, LEAVES * RHS, 128), F32),
            pltpu.SemaphoreType.DMA((4, LEAVES // GROUP)),
        ],
        compiler_params=pltpu.CompilerParams(vmem_limit_bytes=24 * MIB),
        name="outgoing",
    )(*in_hbm(*arrays))


def near_kernel(near_list, base, charges, before, after, blocks, out, sources, blocks_v, sems):
    copies = []
    for g in range(LEAVES // GROUP):
        part = pl.ds(g * GROUP, GROUP)
        copies.append(pltpu.make_async_copy(blocks.at[part], blocks_v.at[part], sems.at[g]))
        copies[-1].start()
    sources[0:LEAVES] = before[...]
    sources[LEAVES : 2 * LEAVES] = charges[...]
    sources[2 * LEAVES : 3 * LEAVES] = after[...]
    half = POINTS // 2
    for g in range(LEAVES // GROUP):
        copies[g].wait()
        for l in range(g * GROUP, (g + 1) * GROUP):
            picked = [sources[near_list[j, l] - base[0]] for j in range(NNEAR)]
            for at in (0, half):
                terms = [dot(picked[j], blocks_v[l, j, at : at + half], NT) for j in range(NNEAR)]
                out[l, :, at : at + half] = sum(terms[1:], terms[0])


def near(near_list, base, charges, before, after, near_blocks):
    vmem = pl.BlockSpec(memory_space=pltpu.VMEM)
    smem = pl.BlockSpec(memory_space=pltpu.SMEM)
    hbm = pl.BlockSpec(memory_space=pltpu.HBM)
    return pl.pallas_call(
        near_kernel,
        out_shape=jax.ShapeDtypeStruct((LEAVES, RHS, POINTS), F32),
        in_specs=[smem, smem, vmem, vmem, vmem, hbm],
        out_specs=vmem,
        scratch_shapes=[
            pltpu.VMEM((3 * LEAVES, RHS, POINTS), BF16),
            pltpu.VMEM(near_blocks.shape, BF16),
            pltpu.SemaphoreType.DMA((LEAVES // GROUP,)),
        ],
        compiler_params=pltpu.CompilerParams(vmem_limit_bytes=32 * MIB),
        cost_estimate=pl.CostEstimate(flops=268435456, bytes_accessed=17000000, transcendentals=0),
        name="near",
    )(near_list.T, base, charges, before, after, *in_hbm(near_blocks))


def unfold(rows):
    return jnp.concatenate([rows[:, :RANK], rows[:, RANK:]], axis=0)


def final_kernel(coarse_list, recv, near_field, target_basis, couplings, transfer, out):
    coarse = jnp.zeros((RHS, RANK), F32)
    for j in range(NCOARSE):
        picked = unfold(recv[coarse_list[0, j], 2].astype(F32)[:4]).astype(BF16)
        coarse += dot(picked, couplings[0, j], NT)
    lowered = dot(coarse.astype(BF16), transfer[...].reshape(LEAVES * RANK, RANK), NT)

    far = jnp.zeros((128, 128), F32)
    span = 32
    lane = iota((span, 8, 128), 2)
    place = iota((span, 8, 128), 1)
    for at in range(0, DEVICES, span):
        part = pl.ds(at, span)
        names = recv[part, 2].astype(F32)
        names = jnp.where(place >= 4, names, pltpu.roll(names, 4, 1)).astype(jnp.int32) - 1
        same = names == lane // 4
        for g in range(2):
            chosen = (same & (lane % 4 == 2 * g + place // 4)).astype(F32)
            far += dot(
                chosen.reshape(span * 8, 128).astype(BF16), recv[part, g].reshape(span * 8, 128), TN
            )
    for l in range(LEAVES):
        rows = unfold(far[l * 4 : (l + 1) * 4, :])
        local = (rows + lowered[:, l * RANK : (l + 1) * RANK]).astype(BF16)
        out[l] = near_field[l] + dot(local, target_basis[l])


def final(coarse_list, recv, near_field, target_basis, coarse_couplings, down_transfer):
    vmem = pl.BlockSpec(memory_space=pltpu.VMEM)
    smem = pl.BlockSpec(memory_space=pltpu.SMEM)
    return pl.pallas_call(
        final_kernel,
        out_shape=jax.ShapeDtypeStruct((LEAVES, RHS, POINTS), F32),
        in_specs=[smem, vmem, vmem, vmem, vmem, vmem],
        out_specs=vmem,
        compiler_params=pltpu.CompilerParams(vmem_limit_bytes=24 * MIB),
        name="final",
    )(coarse_list, recv, near_field, target_basis, coarse_couplings, down_transfer)


def body(
    charges,
    near_list,
    near_blocks,
    source_basis,
    target_basis,
    far_devices,
    far_slots,
    far_couplings,
    up_transfer,
    coarse_list,
    coarse_couplings,
    down_transfer,
):
    count = lax.axis_size(AXES)
    myself = lax.axis_index(AXES)
    up = [(i, i + 1) for i in range(count - 1)]
    down = [(j, i) for i, j in up]
    send = outgoing(charges, far_devices, far_slots, source_basis, far_couplings, up_transfer)
    before = lax.ppermute(charges, AXES, up)
    after = lax.ppermute(charges, AXES, down)
    send, before, after = lax.optimization_barrier((send, before, after))
    recv = lax.all_to_all(send, AXES, 0, 0, tiled=True)
    base = jnp.full((1,), myself * LEAVES - LEAVES, jnp.int32)
    near_field = near(near_list, base, charges, before, after, near_blocks)
    return final(coarse_list, recv, near_field, target_basis, coarse_couplings, down_transfer)


def solution(mesh):
    return jax.shard_map(
        body,
        mesh=mesh,
        in_specs=(P(AXES),) * 12,
        out_specs=P(AXES),
        check_vma=False,
    )
```

```python
import jax
import jax.numpy as jnp
from jax import lax
from jax.experimental import pallas as pl
from jax.experimental.pallas import tpu as pltpu
from jax.sharding import PartitionSpec as P

AXES = ("grp", "dev")
LEAVES = 32
RHS = 8
RANK = 64
POINTS = 256
NFAR = 8
NNEAR = 4
NCOARSE = 6
DEVICES = 128
BF16 = jnp.bfloat16
F32 = jnp.float32
NT = (((1,), (1,)), ((), ()))
TN = (((0,), (0,)), ((), ()))
MIB = 1 << 20
NEAR_FLOPS = 26843545600
NEAR_BYTES = 170000000


def dot(a, b, dims=(((1,), (0,)), ((), ()))):
    return lax.dot_general(a, b, dims, preferred_element_type=F32)


def iota(shape, dim):
    return lax.broadcasted_iota(jnp.int32, shape, dim)


GROUP = 4
CHUNKS = ((0, 16), (16, 32))


def in_hbm(*arrays):
    return tuple(pltpu.with_memory_space_constraint(array, pltpu.HBM) for array in arrays)


def outgoing_kernel(
    charges,
    devices,
    slots,
    basis,
    couplings,
    transfer,
    send,
    charges_v,
    devices_v,
    slots_v,
    basis_v,
    couplings_v,
    transfer_v,
    products,
    chosen,
    sems,
):
    small = [
        pltpu.make_async_copy(src, dst, sems.at[i])
        for i, (src, dst) in enumerate(
            (
                (charges, charges_v),
                (basis, basis_v),
                (devices, devices_v),
                (slots, slots_v),
                (transfer, transfer_v),
            )
        )
    ]
    for copy in small:
        copy.start()
    copies = [
        pltpu.make_async_copy(couplings.at[low:high], couplings_v.at[low:high], sems.at[len(small) + g])
        for g, (low, high) in enumerate(CHUNKS)
    ]
    for copy in copies:
        copy.start()
    small[2].wait()
    small[3].wait()

    entries = LEAVES * NFAR
    device = jnp.concatenate([devices_v[j : j + 1, :] for j in range(NFAR)], axis=1)
    slot = jnp.concatenate([slots_v[j : j + 1, :] for j in range(NFAR)], axis=1)
    named = iota((DEVICES, entries), 0) == device
    earlier = iota((entries, entries), 0) < iota((entries, entries), 1)
    counts = dot(named.astype(BF16), earlier.astype(BF16))
    order = jnp.sum(jnp.where(named, counts, 0.0), axis=0, keepdims=True).astype(jnp.int32)
    row_of = device * 8 + order
    slot_rows = jnp.broadcast_to((slot + 1).astype(F32), (128, entries)).astype(BF16)
    span = 256
    for at in range(0, DEVICES * 8, span):
        row = iota((span, entries), 0) + at
        chosen[at : at + span, :entries] = (row == row_of).astype(BF16)
        chosen[at : at + span, entries:] = (row == row_of + 4).astype(BF16)

    small[0].wait()
    small[1].wait()
    moments = []
    for at in range(0, LEAVES, 4):
        own = charges_v[at : at + 4].reshape(4 * RHS, POINTS)
        product = dot(own, basis_v[at : at + 4].reshape(4 * RANK, POINTS), NT)
        for i in range(4):
            moments.append(product[i * RHS : (i + 1) * RHS, i * RANK : (i + 1) * RANK].astype(BF16))
    small[4].wait()
    raised = []
    for at in range(0, LEAVES, 4):
        product = dot(
            jnp.concatenate(moments[at : at + 4], axis=0),
            transfer_v[at : at + 4].reshape(4 * RANK, RANK),
            NT,
        )
        raised += [product[i * RHS : (i + 1) * RHS, i * RANK : (i + 1) * RANK] for i in range(4)]
    while len(raised) > 1:
        raised = [a + b for a, b in zip(raised[::2], raised[1::2])]
    node = raised[0]
    wide = jnp.concatenate([node, jnp.zeros((RHS, RANK), F32)], axis=1)
    turned = pltpu.roll(pltpu.roll(wide, RANK, 1), 4, 0)
    upper = iota((RHS, 128), 0) < 4
    node_rows = jnp.where(upper, jnp.where(iota((RHS, 128), 1) < RANK, wide, turned), 0.0)
    for at in range(0, DEVICES * 8, span):
        names = dot(chosen[at : at + span, entries:], slot_rows, NT).reshape(span // 8, 8, 128)
        send[at // 8 : (at + span) // 8, 2] = (names + node_rows[None]).astype(BF16)

    for copy, (low, high) in zip(copies, CHUNKS):
        copy.wait()
        for l in range(low, high):
            for h in range(2):
                half = couplings_v[l, h * 4 : h * 4 + 4].reshape(4 * RANK, RANK)
                product = dot(moments[l], half, NT)
                for t in range(2):
                    products[2 * h + t, l * RHS : (l + 1) * RHS, :] = product[:, t * 128 : (t + 1) * 128]

    low = iota((LEAVES, 128), 1) < RANK
    pieces = []
    for c in range(4):
        piece = []
        for t in range(NFAR // 2):
            first = products[t, pl.ds(c, LEAVES, stride=RHS), :]
            second = products[t, pl.ds(c + 4, LEAVES, stride=RHS), :]
            piece.append(jnp.where(low, first, pltpu.roll(second, RANK, 1)))
            piece.append(jnp.where(low, pltpu.roll(first, RANK, 1), second))
        pieces.append(jnp.concatenate(piece, axis=0).astype(BF16))
    table = jnp.concatenate(
        [
            jnp.concatenate([pieces[0], pieces[2]], axis=1),
            jnp.concatenate([pieces[1], pieces[3]], axis=1),
        ],
        axis=0,
    )
    for at in range(0, DEVICES * 8, span):
        rows = dot(chosen[at : at + span, :], table)
        part = pl.ds(at // 8, span // 8)
        send[part, 0] = rows[:, :128].reshape(span // 8, 8, 128).astype(BF16)
        send[part, 1] = rows[:, 128:].reshape(span // 8, 8, 128).astype(BF16)


def outgoing(charges, far_devices, far_slots, source_basis, far_couplings, up_transfer):
    arrays = (charges, far_devices.T, far_slots.T, source_basis, far_couplings, up_transfer)
    return pl.pallas_call(
        outgoing_kernel,
        out_shape=jax.ShapeDtypeStruct((DEVICES, 3, 8, 128), BF16),
        in_specs=[pl.BlockSpec(memory_space=pltpu.HBM)] * 6,
        out_specs=pl.BlockSpec(memory_space=pltpu.VMEM),
        scratch_shapes=[pltpu.VMEM(array.shape, array.dtype) for array in arrays]
        + [
            pltpu.VMEM((NFAR // 2, LEAVES * RHS, 128), F32),
            pltpu.VMEM((DEVICES * 8, 2 * LEAVES * NFAR), BF16),
            pltpu.SemaphoreType.DMA((5 + len(CHUNKS),)),
        ],
        compiler_params=pltpu.CompilerParams(vmem_limit_bytes=24 * MIB),
        cost_estimate=pl.CostEstimate(flops=2684354560, bytes_accessed=60000000, transcendentals=0),
        name="outgoing",
    )(*in_hbm(*arrays))


def near_kernel(near_list, place, charges, first, second, blocks, out, sources, blocks_v, sems):
    own = pltpu.make_async_copy(charges, sources.at[pl.ds(LEAVES, LEAVES)], sems.at[LEAVES // GROUP])
    own.start()
    copies = []
    for g in range(LEAVES // GROUP):
        part = pl.ds(g * GROUP, GROUP)
        copies.append(pltpu.make_async_copy(blocks.at[part], blocks_v.at[part], sems.at[g]))
        copies[-1].start()
    base, parity = place[0], place[1]
    sources[pl.ds((1 - parity) * 2 * LEAVES, LEAVES)] = first[...]
    sources[pl.ds(parity * 2 * LEAVES, LEAVES)] = second[...]
    own.wait()
    half = POINTS // 2
    for g in range(LEAVES // GROUP):
        copies[g].wait()
        for l in range(g * GROUP, (g + 1) * GROUP):
            picked = [sources[near_list[j, l] - base] for j in range(NNEAR)]
            for at in (0, half):
                terms = [dot(picked[j], blocks_v[l, j, at : at + half], NT) for j in range(NNEAR)]
                out[l, :, at : at + half] = sum(terms[1:], terms[0])


def near(near_list, place, charges, first, second, near_blocks):
    vmem = pl.BlockSpec(memory_space=pltpu.VMEM)
    smem = pl.BlockSpec(memory_space=pltpu.SMEM)
    hbm = pl.BlockSpec(memory_space=pltpu.HBM)
    near_list, charges, near_blocks = in_hbm(near_list.T, charges, near_blocks)
    return pl.pallas_call(
        near_kernel,
        out_shape=jax.ShapeDtypeStruct((LEAVES, RHS, POINTS), F32),
        in_specs=[smem, smem, hbm, vmem, vmem, hbm],
        out_specs=vmem,
        scratch_shapes=[
            pltpu.VMEM((3 * LEAVES, RHS, POINTS), BF16),
            pltpu.VMEM(near_blocks.shape, BF16),
            pltpu.SemaphoreType.DMA((LEAVES // GROUP + 1,)),
        ],
        compiler_params=pltpu.CompilerParams(vmem_limit_bytes=32 * MIB),
        cost_estimate=pl.CostEstimate(flops=NEAR_FLOPS, bytes_accessed=NEAR_BYTES, transcendentals=0),
        name="near",
    )(near_list, place, charges, first, second, near_blocks)


def unfold(rows):
    return jnp.concatenate([rows[:, :RANK], rows[:, RANK:]], axis=0)


def final_kernel(coarse_list, recv, near_field, target_basis, couplings, transfer, out):
    coarse = jnp.zeros((RHS, RANK), F32)
    for j in range(NCOARSE):
        picked = unfold(recv[coarse_list[0, j], 2].astype(F32)[:4]).astype(BF16)
        coarse += dot(picked, couplings[0, j], NT)
    lowered = dot(coarse.astype(BF16), transfer[...].reshape(LEAVES * RANK, RANK), NT)

    far = jnp.zeros((128, 128), F32)
    span = 32
    lane = iota((span, 8, 128), 2)
    place = iota((span, 8, 128), 1)
    for at in range(0, DEVICES, span):
        part = pl.ds(at, span)
        names = recv[part, 2].astype(F32)
        names = jnp.where(place >= 4, names, pltpu.roll(names, 4, 1)).astype(jnp.int32) - 1
        same = names == lane // 4
        for g in range(2):
            chosen = (same & (lane % 4 == 2 * g + place // 4)).astype(F32)
            far += dot(
                chosen.reshape(span * 8, 128).astype(BF16), recv[part, g].reshape(span * 8, 128), TN
            )
    for l in range(LEAVES):
        rows = unfold(far[l * 4 : (l + 1) * 4, :])
        local = (rows + lowered[:, l * RANK : (l + 1) * RANK]).astype(BF16)
        out[l] = near_field[l] + dot(local, target_basis[l])


def final(coarse_list, recv, near_field, target_basis, coarse_couplings, down_transfer):
    vmem = pl.BlockSpec(memory_space=pltpu.VMEM)
    smem = pl.BlockSpec(memory_space=pltpu.SMEM)
    return pl.pallas_call(
        final_kernel,
        out_shape=jax.ShapeDtypeStruct((LEAVES, RHS, POINTS), F32),
        in_specs=[smem, vmem, vmem, vmem, vmem, vmem],
        out_specs=vmem,
        compiler_params=pltpu.CompilerParams(vmem_limit_bytes=24 * MIB),
        name="final",
    )(coarse_list, recv, near_field, target_basis, coarse_couplings, down_transfer)


def body(
    charges,
    near_list,
    near_blocks,
    source_basis,
    target_basis,
    far_devices,
    far_slots,
    far_couplings,
    up_transfer,
    coarse_list,
    coarse_couplings,
    down_transfer,
):
    count = lax.axis_size(AXES)
    myself = lax.axis_index(AXES)
    pairs = [[(i, i + 1) for i in range(start, count - 1, 2)] for start in (0, 1)]
    first, second = [
        lax.ppermute(charges, AXES, some + [(j, i) for i, j in some]) for some in pairs
    ]
    send = outgoing(charges, far_devices, far_slots, source_basis, far_couplings, up_transfer)
    recv = lax.all_to_all(send, AXES, 0, 0, tiled=True)
    place = jnp.stack([myself * LEAVES - LEAVES, myself % 2])
    near_field = near(near_list, place, charges, first, second, near_blocks)
    return final(coarse_list, recv, near_field, target_basis, coarse_couplings, down_transfer)


def solution(mesh):
    return jax.shard_map(
        body,
        mesh=mesh,
        in_specs=(P(AXES),) * 12,
        out_specs=P(AXES),
        check_vma=False,
    )
```

```python
import jax
import jax.numpy as jnp
from jax import lax
from jax.experimental import pallas as pl
from jax.experimental.pallas import tpu as pltpu
from jax.sharding import PartitionSpec as P

AXES = ("grp", "dev")
LEAVES = 32
RHS = 8
RANK = 64
POINTS = 256
NFAR = 8
NNEAR = 4
NCOARSE = 6
DEVICES = 128
BF16 = jnp.bfloat16
F32 = jnp.float32
NT = (((1,), (1,)), ((), ()))
TN = (((0,), (0,)), ((), ()))
MIB = 1 << 20
TRIANGLE_FLOPS = 26843545600
NEAR_FLOPS = 26843545600
NEAR_BYTES = 1000


def dot(a, b, dims=(((1,), (0,)), ((), ()))):
    return lax.dot_general(a, b, dims, preferred_element_type=F32)


def iota(shape, dim):
    return lax.broadcasted_iota(jnp.int32, shape, dim)


WRITE = 512
GROUP = 4


def in_hbm(*arrays):
    return tuple(pltpu.with_memory_space_constraint(array, pltpu.HBM) for array in arrays)


def triangle_kernel(earlier):
    earlier[...] = (iota(earlier.shape, 0) < iota(earlier.shape, 1)).astype(BF16)


def triangle():
    entries = LEAVES * NFAR
    return pl.pallas_call(
        triangle_kernel,
        out_shape=jax.ShapeDtypeStruct((entries, entries), BF16),
        out_specs=pl.BlockSpec(memory_space=pltpu.VMEM),
        compiler_params=pltpu.CompilerParams(vmem_limit_bytes=8 * MIB),
        cost_estimate=pl.CostEstimate(flops=TRIANGLE_FLOPS, bytes_accessed=1000, transcendentals=0),
        name="triangle",
    )()


def outgoing_kernel(
    earlier, devices, slots, charges, basis, couplings, transfer, send_hbm, send, products, sems
):
    entries = LEAVES * NFAR
    device = jnp.concatenate([devices[j : j + 1, :] for j in range(NFAR)], axis=1)
    slot = jnp.concatenate([slots[j : j + 1, :] for j in range(NFAR)], axis=1)
    named = iota((DEVICES, entries), 0) == device
    counts = dot(named.astype(BF16), earlier[...])
    order = jnp.sum(jnp.where(named, counts, 0.0), axis=0, keepdims=True).astype(jnp.int32)
    row_of = device * 8 + order
    slot_rows = jnp.broadcast_to((slot + 1).astype(F32), (128, entries)).astype(BF16)

    moments = []
    for at in range(0, LEAVES, 4):
        own = charges[at : at + 4].reshape(4 * RHS, POINTS)
        product = dot(own, basis[at : at + 4].reshape(4 * RANK, POINTS), NT)
        for i in range(4):
            moments.append(product[i * RHS : (i + 1) * RHS, i * RANK : (i + 1) * RANK].astype(BF16))
    raised = []
    for at in range(0, LEAVES, 4):
        product = dot(
            jnp.concatenate(moments[at : at + 4], axis=0),
            transfer[at : at + 4].reshape(4 * RANK, RANK),
            NT,
        )
        raised += [product[i * RHS : (i + 1) * RHS, i * RANK : (i + 1) * RANK] for i in range(4)]
    while len(raised) > 1:
        raised = [a + b for a, b in zip(raised[::2], raised[1::2])]
    node = raised[0]

    wide = jnp.concatenate([node, jnp.zeros((RHS, RANK), F32)], axis=1)
    turned = pltpu.roll(pltpu.roll(wide, RANK, 1), 4, 0)
    upper = iota((RHS, 128), 0) < 4
    node_rows = jnp.where(upper, jnp.where(iota((RHS, 128), 1) < RANK, wide, turned), 0.0)

    span = 256
    for at in range(0, DEVICES * 8, span):
        second = (iota((span, entries), 0) + at == row_of + 4).astype(BF16)
        names = dot(second, slot_rows, NT).reshape(span // 8, 8, 128) + node_rows[None]
        send[at // 8 : (at + span) // 8, 2] = names.astype(BF16)
    writes = [pltpu.make_async_copy(send.at[:, 2], send_hbm.at[:, 2], sems.at[0])]
    writes[0].start()

    for l in range(LEAVES):
        for h in range(2):
            half = couplings[l, h * 4 : h * 4 + 4].reshape(4 * RANK, RANK)
            product = dot(moments[l], half, NT)
            for t in range(2):
                products[2 * h + t, l * RHS : (l + 1) * RHS, :] = product[:, t * 128 : (t + 1) * 128]

    low = iota((LEAVES, 128), 1) < RANK
    pieces = []
    for c in range(4):
        piece = []
        for t in range(NFAR // 2):
            first = products[t, pl.ds(c, LEAVES, stride=RHS), :]
            second = products[t, pl.ds(c + 4, LEAVES, stride=RHS), :]
            piece.append(jnp.where(low, first, pltpu.roll(second, RANK, 1)))
            piece.append(jnp.where(low, pltpu.roll(first, RANK, 1), second))
        pieces.append(jnp.concatenate(piece, axis=0).astype(BF16))
    table = jnp.concatenate(
        [
            jnp.concatenate([pieces[0], pieces[2]], axis=1),
            jnp.concatenate([pieces[1], pieces[3]], axis=1),
        ],
        axis=0,
    )
    for at in range(0, DEVICES * 8, span):
        row = iota((span, entries), 0) + at
        chosen = (row == row_of).astype(BF16)
        second = (row == row_of + 4).astype(BF16)
        rows = dot(jnp.concatenate([chosen, second], axis=1), table)
        part = pl.ds(at // 8, span // 8)
        send[part, 0] = rows[:, :128].reshape(span // 8, 8, 128).astype(BF16)
        send[part, 1] = rows[:, 128:].reshape(span // 8, 8, 128).astype(BF16)
        if (at + span) % WRITE == 0:
            part = pl.ds((at + span - WRITE) // 8, WRITE // 8)
            writes.append(
                pltpu.make_async_copy(send.at[part, 0:2], send_hbm.at[part, 0:2], sems.at[len(writes)])
            )
            writes[-1].start()
    for write in writes:
        write.wait()


def outgoing(earlier, far_devices, far_slots, charges, source_basis, far_couplings, up_transfer):
    vmem = pl.BlockSpec(memory_space=pltpu.VMEM)
    return pl.pallas_call(
        outgoing_kernel,
        out_shape=jax.ShapeDtypeStruct((DEVICES, 3, 8, 128), BF16),
        in_specs=[vmem] * 7,
        out_specs=pl.BlockSpec(memory_space=pltpu.HBM),
        scratch_shapes=[
            pltpu.VMEM((DEVICES, 3, 8, 128), BF16),
            pltpu.VMEM((NFAR // 2, LEAVES * RHS, 128), F32),
            pltpu.SemaphoreType.DMA((1 + DEVICES * 8 // WRITE,)),
        ],
        compiler_params=pltpu.CompilerParams(vmem_limit_bytes=24 * MIB),
        cost_estimate=pl.CostEstimate(flops=26843545600, bytes_accessed=1000, transcendentals=0),
        name="outgoing",
    )(earlier, far_devices.T, far_slots.T, charges, source_basis, far_couplings, up_transfer)


def near_kernel(near_list, place, charges, first, second, blocks, out, sources, blocks_v, sems):
    own = pltpu.make_async_copy(charges, sources.at[pl.ds(LEAVES, LEAVES)], sems.at[LEAVES // GROUP])
    own.start()
    copies = []
    for g in range(LEAVES // GROUP):
        part = pl.ds(g * GROUP, GROUP)
        copies.append(pltpu.make_async_copy(blocks.at[part], blocks_v.at[part], sems.at[g]))
        copies[-1].start()
    base, parity = place[0], place[1]
    sources[pl.ds((1 - parity) * 2 * LEAVES, LEAVES)] = first[...]
    sources[pl.ds(parity * 2 * LEAVES, LEAVES)] = second[...]
    own.wait()
    half = POINTS // 2
    for g in range(LEAVES // GROUP):
        copies[g].wait()
        for l in range(g * GROUP, (g + 1) * GROUP):
            picked = [sources[near_list[j, l] - base] for j in range(NNEAR)]
            for at in (0, half):
                terms = [dot(picked[j], blocks_v[l, j, at : at + half], NT) for j in range(NNEAR)]
                out[l, :, at : at + half] = sum(terms[1:], terms[0])


def near(near_list, place, charges, first, second, near_blocks):
    vmem = pl.BlockSpec(memory_space=pltpu.VMEM)
    smem = pl.BlockSpec(memory_space=pltpu.SMEM)
    hbm = pl.BlockSpec(memory_space=pltpu.HBM)
    near_list, charges, near_blocks = in_hbm(near_list.T, charges, near_blocks)
    return pl.pallas_call(
        near_kernel,
        out_shape=jax.ShapeDtypeStruct((LEAVES, RHS, POINTS), F32),
        in_specs=[smem, smem, hbm, vmem, vmem, hbm],
        out_specs=vmem,
        scratch_shapes=[
            pltpu.VMEM((3 * LEAVES, RHS, POINTS), BF16),
            pltpu.VMEM(near_blocks.shape, BF16),
            pltpu.SemaphoreType.DMA((LEAVES // GROUP + 1,)),
        ],
        compiler_params=pltpu.CompilerParams(vmem_limit_bytes=32 * MIB),
        cost_estimate=pl.CostEstimate(flops=NEAR_FLOPS, bytes_accessed=NEAR_BYTES, transcendentals=0),
        name="near",
    )(near_list, place, charges, first, second, near_blocks)


def unfold(rows):
    return jnp.concatenate([rows[:, :RANK], rows[:, RANK:]], axis=0)


def final_kernel(coarse_list, recv, near_field, target_basis, couplings, transfer, out):
    coarse = jnp.zeros((RHS, RANK), F32)
    for j in range(NCOARSE):
        picked = unfold(recv[coarse_list[0, j], 2].astype(F32)[:4]).astype(BF16)
        coarse += dot(picked, couplings[0, j], NT)
    lowered = dot(coarse.astype(BF16), transfer[...].reshape(LEAVES * RANK, RANK), NT)

    far = jnp.zeros((128, 128), F32)
    span = 32
    lane = iota((span, 8, 128), 2)
    place = iota((span, 8, 128), 1)
    for at in range(0, DEVICES, span):
        part = pl.ds(at, span)
        names = recv[part, 2].astype(F32)
        names = jnp.where(place >= 4, names, pltpu.roll(names, 4, 1)).astype(jnp.int32) - 1
        same = names == lane // 4
        for g in range(2):
            chosen = (same & (lane % 4 == 2 * g + place // 4)).astype(F32)
            far += dot(
                chosen.reshape(span * 8, 128).astype(BF16), recv[part, g].reshape(span * 8, 128), TN
            )
    for l in range(LEAVES):
        rows = unfold(far[l * 4 : (l + 1) * 4, :])
        local = (rows + lowered[:, l * RANK : (l + 1) * RANK]).astype(BF16)
        out[l] = near_field[l] + dot(local, target_basis[l])


def final(coarse_list, recv, near_field, target_basis, coarse_couplings, down_transfer):
    vmem = pl.BlockSpec(memory_space=pltpu.VMEM)
    smem = pl.BlockSpec(memory_space=pltpu.SMEM)
    return pl.pallas_call(
        final_kernel,
        out_shape=jax.ShapeDtypeStruct((LEAVES, RHS, POINTS), F32),
        in_specs=[smem, vmem, vmem, vmem, vmem, vmem],
        out_specs=vmem,
        compiler_params=pltpu.CompilerParams(vmem_limit_bytes=24 * MIB),
        name="final",
    )(coarse_list, recv, near_field, target_basis, coarse_couplings, down_transfer)


def body(
    charges,
    near_list,
    near_blocks,
    source_basis,
    target_basis,
    far_devices,
    far_slots,
    far_couplings,
    up_transfer,
    coarse_list,
    coarse_couplings,
    down_transfer,
):
    count = lax.axis_size(AXES)
    myself = lax.axis_index(AXES)
    pairs = [[(i, i + 1) for i in range(start, count - 1, 2)] for start in (0, 1)]
    earlier, mine = lax.optimization_barrier((triangle(), charges))
    exchange = [some + [(j, i) for i, j in some] for some in pairs]
    first = lax.ppermute(charges, AXES, exchange[0])
    second = lax.ppermute(mine, AXES, exchange[1])
    send = outgoing(earlier, far_devices, far_slots, charges, source_basis, far_couplings, up_transfer)
    recv = lax.all_to_all(send, AXES, 0, 0, tiled=True)
    place = jnp.stack([myself * LEAVES - LEAVES, myself % 2])
    near_field = near(near_list, place, charges, first, second, near_blocks)
    return final(coarse_list, recv, near_field, target_basis, coarse_couplings, down_transfer)


def solution(mesh):
    return jax.shard_map(
        body,
        mesh=mesh,
        in_specs=(P(AXES),) * 12,
        out_specs=P(AXES),
        check_vma=False,
    )
```

```python
import jax
import jax.numpy as jnp
from jax import lax
from jax.experimental import pallas as pl
from jax.experimental.pallas import tpu as pltpu
from jax.sharding import PartitionSpec as P

AXES = ("grp", "dev")
LEAVES = 32
RHS = 8
RANK = 64
POINTS = 256
NFAR = 8
NNEAR = 4
NCOARSE = 6
DEVICES = 128
BF16 = jnp.bfloat16
F32 = jnp.float32
NT = (((1,), (1,)), ((), ()))
TN = (((0,), (0,)), ((), ()))
MIB = 1 << 20
TRIANGLE_FLOPS = 26843545600
NEAR_FLOPS = 4600000000


def dot(a, b, dims=(((1,), (0,)), ((), ()))):
    return lax.dot_general(a, b, dims, preferred_element_type=F32)


def iota(shape, dim):
    return lax.broadcasted_iota(jnp.int32, shape, dim)


WRITE = 512


def in_hbm(*arrays):
    return tuple(pltpu.with_memory_space_constraint(array, pltpu.HBM) for array in arrays)


def triangle_kernel(earlier):
    earlier[...] = (iota(earlier.shape, 0) < iota(earlier.shape, 1)).astype(BF16)


def triangle():
    entries = LEAVES * NFAR
    return pl.pallas_call(
        triangle_kernel,
        out_shape=jax.ShapeDtypeStruct((entries, entries), BF16),
        out_specs=pl.BlockSpec(memory_space=pltpu.VMEM),
        compiler_params=pltpu.CompilerParams(vmem_limit_bytes=8 * MIB),
        cost_estimate=pl.CostEstimate(flops=TRIANGLE_FLOPS, bytes_accessed=1000, transcendentals=0),
        name="triangle",
    )()


def outgoing_kernel(
    earlier, devices, slots, charges, basis, couplings, transfer, send_hbm, send, products, sems
):
    entries = LEAVES * NFAR
    device = jnp.concatenate([devices[j : j + 1, :] for j in range(NFAR)], axis=1)
    slot = jnp.concatenate([slots[j : j + 1, :] for j in range(NFAR)], axis=1)
    named = iota((DEVICES, entries), 0) == device
    counts = dot(named.astype(BF16), earlier[...])
    order = jnp.sum(jnp.where(named, counts, 0.0), axis=0, keepdims=True).astype(jnp.int32)
    row_of = device * 8 + order
    slot_rows = jnp.broadcast_to((slot + 1).astype(F32), (128, entries)).astype(BF16)

    moments = []
    for at in range(0, LEAVES, 4):
        own = charges[at : at + 4].reshape(4 * RHS, POINTS)
        product = dot(own, basis[at : at + 4].reshape(4 * RANK, POINTS), NT)
        for i in range(4):
            moments.append(product[i * RHS : (i + 1) * RHS, i * RANK : (i + 1) * RANK].astype(BF16))
    raised = []
    for at in range(0, LEAVES, 4):
        product = dot(
            jnp.concatenate(moments[at : at + 4], axis=0),
            transfer[at : at + 4].reshape(4 * RANK, RANK),
            NT,
        )
        raised += [product[i * RHS : (i + 1) * RHS, i * RANK : (i + 1) * RANK] for i in range(4)]
    while len(raised) > 1:
        raised = [a + b for a, b in zip(raised[::2], raised[1::2])]
    node = raised[0]

    wide = jnp.concatenate([node, jnp.zeros((RHS, RANK), F32)], axis=1)
    turned = pltpu.roll(pltpu.roll(wide, RANK, 1), 4, 0)
    upper = iota((RHS, 128), 0) < 4
    node_rows = jnp.where(upper, jnp.where(iota((RHS, 128), 1) < RANK, wide, turned), 0.0)

    span = 256
    for at in range(0, DEVICES * 8, span):
        second = (iota((span, entries), 0) + at == row_of + 4).astype(BF16)
        names = dot(second, slot_rows, NT).reshape(span // 8, 8, 128) + node_rows[None]
        send[at // 8 : (at + span) // 8, 2] = names.astype(BF16)
    writes = [pltpu.make_async_copy(send.at[:, 2], send_hbm.at[:, 2], sems.at[0])]
    writes[0].start()

    for l in range(LEAVES):
        for h in range(2):
            half = couplings[l, h * 4 : h * 4 + 4].reshape(4 * RANK, RANK)
            product = dot(moments[l], half, NT)
            for t in range(2):
                products[2 * h + t, l * RHS : (l + 1) * RHS, :] = product[:, t * 128 : (t + 1) * 128]

    low = iota((LEAVES, 128), 1) < RANK
    pieces = []
    for c in range(4):
        piece = []
        for t in range(NFAR // 2):
            first = products[t, pl.ds(c, LEAVES, stride=RHS), :]
            second = products[t, pl.ds(c + 4, LEAVES, stride=RHS), :]
            piece.append(jnp.where(low, first, pltpu.roll(second, RANK, 1)))
            piece.append(jnp.where(low, pltpu.roll(first, RANK, 1), second))
        pieces.append(jnp.concatenate(piece, axis=0).astype(BF16))
    table = jnp.concatenate(
        [
            jnp.concatenate([pieces[0], pieces[2]], axis=1),
            jnp.concatenate([pieces[1], pieces[3]], axis=1),
        ],
        axis=0,
    )
    for at in range(0, DEVICES * 8, span):
        row = iota((span, entries), 0) + at
        chosen = (row == row_of).astype(BF16)
        second = (row == row_of + 4).astype(BF16)
        rows = dot(jnp.concatenate([chosen, second], axis=1), table)
        part = pl.ds(at // 8, span // 8)
        send[part, 0] = rows[:, :128].reshape(span // 8, 8, 128).astype(BF16)
        send[part, 1] = rows[:, 128:].reshape(span // 8, 8, 128).astype(BF16)
        if (at + span) % WRITE == 0:
            part = pl.ds((at + span - WRITE) // 8, WRITE // 8)
            writes.append(
                pltpu.make_async_copy(send.at[part, 0:2], send_hbm.at[part, 0:2], sems.at[len(writes)])
            )
            writes[-1].start()
    for write in writes:
        write.wait()


def outgoing(earlier, far_devices, far_slots, charges, source_basis, far_couplings, up_transfer):
    vmem = pl.BlockSpec(memory_space=pltpu.VMEM)
    return pl.pallas_call(
        outgoing_kernel,
        out_shape=jax.ShapeDtypeStruct((DEVICES, 3, 8, 128), BF16),
        in_specs=[vmem] * 7,
        out_specs=pl.BlockSpec(memory_space=pltpu.HBM),
        scratch_shapes=[
            pltpu.VMEM((DEVICES, 3, 8, 128), BF16),
            pltpu.VMEM((NFAR // 2, LEAVES * RHS, 128), F32),
            pltpu.SemaphoreType.DMA((1 + DEVICES * 8 // WRITE,)),
        ],
        compiler_params=pltpu.CompilerParams(vmem_limit_bytes=24 * MIB),
        cost_estimate=pl.CostEstimate(flops=26843545600, bytes_accessed=1000, transcendentals=0),
        name="outgoing",
    )(earlier, far_devices.T, far_slots.T, charges, source_basis, far_couplings, up_transfer)


def near_terms(near_list, base, sources, blocks, l, js):
    picked = [sources[near_list[j, l] - base] for j in js]
    half = POINTS // 2
    return [
        dot(picked[0], blocks[l, js[0], at : at + half], NT)
        + dot(picked[1], blocks[l, js[1], at : at + half], NT)
        for at in (0, half)
    ]


def near_first_kernel(near_list, place, charges, first, blocks, out, sources):
    base, parity = place[0], place[1]
    sources[LEAVES : 2 * LEAVES] = charges[...]
    sources[pl.ds((1 - parity) * 2 * LEAVES, LEAVES)] = first[...]
    for l in range(LEAVES):
        left, right = near_terms(near_list, base, sources, blocks, l, (0, 2 - parity))
        out[l, :, : POINTS // 2] = left
        out[l, :, POINTS // 2 :] = right


def near_second_kernel(
    near_list, place, charges, first, second, far_second, blocks, partial, out, sources
):
    base, parity = place[0], place[1]
    sources[LEAVES : 2 * LEAVES] = charges[...]
    sources[pl.ds((1 - parity) * 2 * LEAVES, LEAVES)] = first[...]
    sources[pl.ds(parity * 2 * LEAVES, LEAVES)] = second[...] + far_second[...]
    for l in range(LEAVES):
        left, right = near_terms(near_list, base, sources, blocks, l, (1 + parity, NNEAR - 1))
        out[l, :, : POINTS // 2] = partial[l, :, : POINTS // 2] + left
        out[l, :, POINTS // 2 :] = partial[l, :, POINTS // 2 :] + right


def near(kernel, name, near_list, place, *arrays):
    vmem = pl.BlockSpec(memory_space=pltpu.VMEM)
    smem = pl.BlockSpec(memory_space=pltpu.SMEM)
    return pl.pallas_call(
        kernel,
        out_shape=jax.ShapeDtypeStruct((LEAVES, RHS, POINTS), F32),
        in_specs=[smem, smem] + [vmem] * len(arrays),
        out_specs=vmem,
        scratch_shapes=[pltpu.VMEM((3 * LEAVES, RHS, POINTS), BF16)],
        compiler_params=pltpu.CompilerParams(vmem_limit_bytes=20 * MIB),
        cost_estimate=pl.CostEstimate(flops=NEAR_FLOPS, bytes_accessed=1000, transcendentals=0),
        name=name,
    )(*in_hbm(near_list.T), place, *arrays)


def unfold(rows):
    return jnp.concatenate([rows[:, :RANK], rows[:, RANK:]], axis=0)


def final_kernel(coarse_list, recv, near_field, target_basis, couplings, transfer, out):
    coarse = jnp.zeros((RHS, RANK), F32)
    for j in range(NCOARSE):
        picked = unfold(recv[coarse_list[0, j], 2].astype(F32)[:4]).astype(BF16)
        coarse += dot(picked, couplings[0, j], NT)
    lowered = dot(coarse.astype(BF16), transfer[...].reshape(LEAVES * RANK, RANK), NT)

    far = jnp.zeros((128, 128), F32)
    span = 32
    lane = iota((span, 8, 128), 2)
    place = iota((span, 8, 128), 1)
    for at in range(0, DEVICES, span):
        part = pl.ds(at, span)
        names = recv[part, 2].astype(F32)
        names = jnp.where(place >= 4, names, pltpu.roll(names, 4, 1)).astype(jnp.int32) - 1
        same = names == lane // 4
        for g in range(2):
            chosen = (same & (lane % 4 == 2 * g + place // 4)).astype(F32)
            far += dot(
                chosen.reshape(span * 8, 128).astype(BF16), recv[part, g].reshape(span * 8, 128), TN
            )
    for l in range(LEAVES):
        rows = unfold(far[l * 4 : (l + 1) * 4, :])
        local = (rows + lowered[:, l * RANK : (l + 1) * RANK]).astype(BF16)
        out[l] = near_field[l] + dot(local, target_basis[l])


def final(coarse_list, recv, near_field, target_basis, coarse_couplings, down_transfer):
    vmem = pl.BlockSpec(memory_space=pltpu.VMEM)
    smem = pl.BlockSpec(memory_space=pltpu.SMEM)
    return pl.pallas_call(
        final_kernel,
        out_shape=jax.ShapeDtypeStruct((LEAVES, RHS, POINTS), F32),
        in_specs=[smem, vmem, vmem, vmem, vmem, vmem],
        out_specs=vmem,
        compiler_params=pltpu.CompilerParams(vmem_limit_bytes=24 * MIB),
        name="final",
    )(coarse_list, recv, near_field, target_basis, coarse_couplings, down_transfer)


def body(
    charges,
    near_list,
    near_blocks,
    source_basis,
    target_basis,
    far_devices,
    far_slots,
    far_couplings,
    up_transfer,
    coarse_list,
    coarse_couplings,
    down_transfer,
):
    count = lax.axis_size(AXES)
    myself = lax.axis_index(AXES)
    of_subtree = lax.axis_size("dev")
    pairs = [[(i, i + 1) for i in range(start, count - 1, 2)] for start in (0, 1)]
    ends = [(i, j) for i, j in pairs[1] if j % of_subtree == 0]
    inner = [(i, j) for i, j in pairs[1] if j % of_subtree != 0]
    first, far_second = [
        lax.ppermute(charges, AXES, some + [(j, i) for i, j in some]) for some in (pairs[0], ends)
    ]
    earlier, mine = lax.optimization_barrier((triangle(), charges))
    send = outgoing(earlier, far_devices, far_slots, mine, source_basis, far_couplings, up_transfer)
    send, mine = lax.optimization_barrier((send, mine))
    recv = lax.all_to_all(send, AXES, 0, 0, tiled=True)
    second = lax.ppermute(mine, AXES, inner + [(j, i) for i, j in inner])
    place = jnp.stack([myself * LEAVES - LEAVES, myself % 2])
    partial = near(near_first_kernel, "near_first", near_list, place, mine, first, near_blocks)
    near_field = near(
        near_second_kernel,
        "near_second",
        near_list,
        place,
        mine,
        first,
        second,
        far_second,
        near_blocks,
        partial,
    )
    return final(coarse_list, recv, near_field, target_basis, coarse_couplings, down_transfer)


def solution(mesh):
    return jax.shard_map(
        body,
        mesh=mesh,
        in_specs=(P(AXES),) * 12,
        out_specs=P(AXES),
        check_vma=False,
    )
```

```python
import jax
import jax.numpy as jnp
from jax import lax
from jax.experimental import pallas as pl
from jax.experimental.pallas import tpu as pltpu
from jax.sharding import PartitionSpec as P

AXES = ("grp", "dev")
LEAVES = 32
RHS = 8
RANK = 64
POINTS = 256
NFAR = 8
NNEAR = 4
NCOARSE = 6
DEVICES = 128
BF16 = jnp.bfloat16
F32 = jnp.float32
NT = (((1,), (1,)), ((), ()))
TN = (((0,), (0,)), ((), ()))
MIB = 1 << 20
TRIANGLE_FLOPS = 26843545600
NEAR_FLOPS = 4600000000


def dot(a, b, dims=(((1,), (0,)), ((), ()))):
    return lax.dot_general(a, b, dims, preferred_element_type=F32)


def iota(shape, dim):
    return lax.broadcasted_iota(jnp.int32, shape, dim)


WRITE = 512


def in_hbm(*arrays):
    return tuple(pltpu.with_memory_space_constraint(array, pltpu.HBM) for array in arrays)


def triangle_kernel(earlier):
    earlier[...] = (iota(earlier.shape, 0) < iota(earlier.shape, 1)).astype(BF16)


def triangle():
    entries = LEAVES * NFAR
    return pl.pallas_call(
        triangle_kernel,
        out_shape=jax.ShapeDtypeStruct((entries, entries), BF16),
        out_specs=pl.BlockSpec(memory_space=pltpu.VMEM),
        compiler_params=pltpu.CompilerParams(vmem_limit_bytes=8 * MIB),
        cost_estimate=pl.CostEstimate(flops=TRIANGLE_FLOPS, bytes_accessed=1000, transcendentals=0),
        name="triangle",
    )()


def outgoing_kernel(
    earlier, devices, slots, charges, basis, couplings, transfer, send_hbm, send, products, sems
):
    entries = LEAVES * NFAR
    device = jnp.concatenate([devices[j : j + 1, :] for j in range(NFAR)], axis=1)
    slot = jnp.concatenate([slots[j : j + 1, :] for j in range(NFAR)], axis=1)
    named = iota((DEVICES, entries), 0) == device
    counts = dot(named.astype(BF16), earlier[...])
    order = jnp.sum(jnp.where(named, counts, 0.0), axis=0, keepdims=True).astype(jnp.int32)
    row_of = device * 8 + order
    slot_rows = jnp.broadcast_to((slot + 1).astype(F32), (128, entries)).astype(BF16)

    moments = []
    for at in range(0, LEAVES, 4):
        own = charges[at : at + 4].reshape(4 * RHS, POINTS)
        product = dot(own, basis[at : at + 4].reshape(4 * RANK, POINTS), NT)
        for i in range(4):
            moments.append(product[i * RHS : (i + 1) * RHS, i * RANK : (i + 1) * RANK].astype(BF16))
    raised = []
    for at in range(0, LEAVES, 4):
        product = dot(
            jnp.concatenate(moments[at : at + 4], axis=0),
            transfer[at : at + 4].reshape(4 * RANK, RANK),
            NT,
        )
        raised += [product[i * RHS : (i + 1) * RHS, i * RANK : (i + 1) * RANK] for i in range(4)]
    while len(raised) > 1:
        raised = [a + b for a, b in zip(raised[::2], raised[1::2])]
    node = raised[0]

    wide = jnp.concatenate([node, jnp.zeros((RHS, RANK), F32)], axis=1)
    turned = pltpu.roll(pltpu.roll(wide, RANK, 1), 4, 0)
    upper = iota((RHS, 128), 0) < 4
    node_rows = jnp.where(upper, jnp.where(iota((RHS, 128), 1) < RANK, wide, turned), 0.0)

    span = 256
    for at in range(0, DEVICES * 8, span):
        second = (iota((span, entries), 0) + at == row_of + 4).astype(BF16)
        names = dot(second, slot_rows, NT).reshape(span // 8, 8, 128) + node_rows[None]
        send[at // 8 : (at + span) // 8, 2] = names.astype(BF16)
    writes = [pltpu.make_async_copy(send.at[:, 2], send_hbm.at[:, 2], sems.at[0])]
    writes[0].start()

    for l in range(LEAVES):
        for h in range(2):
            half = couplings[l, h * 4 : h * 4 + 4].reshape(4 * RANK, RANK)
            product = dot(moments[l], half, NT)
            for t in range(2):
                products[2 * h + t, l * RHS : (l + 1) * RHS, :] = product[:, t * 128 : (t + 1) * 128]

    low = iota((LEAVES, 128), 1) < RANK
    pieces = []
    for c in range(4):
        piece = []
        for t in range(NFAR // 2):
            first = products[t, pl.ds(c, LEAVES, stride=RHS), :]
            second = products[t, pl.ds(c + 4, LEAVES, stride=RHS), :]
            piece.append(jnp.where(low, first, pltpu.roll(second, RANK, 1)))
            piece.append(jnp.where(low, pltpu.roll(first, RANK, 1), second))
        pieces.append(jnp.concatenate(piece, axis=0).astype(BF16))
    table = jnp.concatenate(
        [
            jnp.concatenate([pieces[0], pieces[2]], axis=1),
            jnp.concatenate([pieces[1], pieces[3]], axis=1),
        ],
        axis=0,
    )
    for at in range(0, DEVICES * 8, span):
        row = iota((span, entries), 0) + at
        chosen = (row == row_of).astype(BF16)
        second = (row == row_of + 4).astype(BF16)
        rows = dot(jnp.concatenate([chosen, second], axis=1), table)
        part = pl.ds(at // 8, span // 8)
        send[part, 0] = rows[:, :128].reshape(span // 8, 8, 128).astype(BF16)
        send[part, 1] = rows[:, 128:].reshape(span // 8, 8, 128).astype(BF16)
        if (at + span) % WRITE == 0:
            part = pl.ds((at + span - WRITE) // 8, WRITE // 8)
            writes.append(
                pltpu.make_async_copy(send.at[part, 0:2], send_hbm.at[part, 0:2], sems.at[len(writes)])
            )
            writes[-1].start()
    for write in writes:
        write.wait()


def outgoing(earlier, far_devices, far_slots, charges, source_basis, far_couplings, up_transfer):
    vmem = pl.BlockSpec(memory_space=pltpu.VMEM)
    return pl.pallas_call(
        outgoing_kernel,
        out_shape=jax.ShapeDtypeStruct((DEVICES, 3, 8, 128), BF16),
        in_specs=[vmem] * 7,
        out_specs=pl.BlockSpec(memory_space=pltpu.HBM),
        scratch_shapes=[
            pltpu.VMEM((DEVICES, 3, 8, 128), BF16),
            pltpu.VMEM((NFAR // 2, LEAVES * RHS, 128), F32),
            pltpu.SemaphoreType.DMA((1 + DEVICES * 8 // WRITE,)),
        ],
        compiler_params=pltpu.CompilerParams(vmem_limit_bytes=24 * MIB),
        cost_estimate=pl.CostEstimate(flops=26843545600, bytes_accessed=1000, transcendentals=0),
        name="outgoing",
    )(earlier, far_devices.T, far_slots.T, charges, source_basis, far_couplings, up_transfer)


def position():
    return lax.axis_index(AXES)


def near_term(source, blocks, l, j):
    half = POINTS // 2
    return [dot(source, blocks[l, j, at : at + half], NT) for at in (0, half)]


def near_first_kernel(charges, first, blocks, out):
    j = 2 - position() % 2
    half = POINTS // 2
    for l in range(LEAVES):
        own = near_term(charges[l], blocks, l, 0)
        other = near_term(first[l], blocks, l, j)
        out[l, :, :half] = own[0] + other[0]
        out[l, :, half:] = own[1] + other[1]


def near_second_kernel(
    near_list, charges, first, second, far_second, blocks, partial, out, sources, listed, sem
):
    copy = pltpu.make_async_copy(near_list, listed, sem)
    copy.start()
    me = position()
    parity = me % 2
    half = POINTS // 2
    edge = jnp.where(me == 0, charges[0], jnp.where(me == DEVICES - 1, charges[LEAVES - 1], 0.0))
    sources[LEAVES : 2 * LEAVES] = charges[...]
    sources[pl.ds((1 - parity) * 2 * LEAVES, LEAVES)] = first[...]
    for l in range(LEAVES):
        source = second[l] + far_second[l]
        sources[parity * 2 * LEAVES + l] = source
        term = near_term(source + edge, blocks, l, 1 + parity)
        out[l, :, :half] = partial[l, :, :half] + term[0]
        out[l, :, half:] = partial[l, :, half:] + term[1]
    copy.wait()
    base = me * LEAVES - LEAVES
    for l in range(LEAVES):
        term = near_term(sources[listed[NNEAR - 1, l] - base], blocks, l, NNEAR - 1)
        out[l, :, :half] += term[0]
        out[l, :, half:] += term[1]


def near(kernel, name, arrays, scratch_shapes=()):
    return pl.pallas_call(
        kernel,
        out_shape=jax.ShapeDtypeStruct((LEAVES, RHS, POINTS), F32),
        in_specs=[pl.BlockSpec(memory_space=pltpu.VMEM)] * len(arrays),
        out_specs=pl.BlockSpec(memory_space=pltpu.VMEM),
        scratch_shapes=scratch_shapes,
        compiler_params=pltpu.CompilerParams(vmem_limit_bytes=20 * MIB),
        cost_estimate=pl.CostEstimate(flops=NEAR_FLOPS, bytes_accessed=1000, transcendentals=0),
        name=name,
    )(*arrays)


def near_first(charges, first, near_blocks):
    return near(near_first_kernel, "near_first", (charges, first, near_blocks))


def near_second(near_list, charges, first, second, far_second, near_blocks, partial):
    return near(
        near_second_kernel,
        "near_second",
        (near_list.T, charges, first, second, far_second, near_blocks, partial),
        (
            pltpu.VMEM((3 * LEAVES, RHS, POINTS), BF16),
            pltpu.SMEM((NNEAR, LEAVES), jnp.int32),
            pltpu.SemaphoreType.DMA,
        ),
    )


def unfold(rows):
    return jnp.concatenate([rows[:, :RANK], rows[:, RANK:]], axis=0)


def final_kernel(coarse_list, recv, near_field, target_basis, couplings, transfer, out):
    shape = (NCOARSE * 4, NCOARSE)
    listed = jnp.where(iota(shape, 0) // 4 == iota(shape, 1), coarse_list[...], 0)
    row_of = jnp.sum(listed, axis=1, keepdims=True) * 8 + iota((NCOARSE * 4, 1), 0) % 4
    chosen = (iota((NCOARSE * 4, DEVICES * 8), 1) == row_of).astype(BF16)
    picked = dot(chosen, recv[:, 2].reshape(DEVICES * 8, 128)).astype(BF16)
    coarse = jnp.zeros((RHS, RANK), F32)
    for j in range(NCOARSE):
        coarse += dot(unfold(picked[4 * j : 4 * j + 4]), couplings[0, j], NT)
    lowered = dot(coarse.astype(BF16), transfer[...].reshape(LEAVES * RANK, RANK), NT)

    far = jnp.zeros((128, 128), F32)
    span = 32
    lane = iota((span, 8, 128), 2)
    place = iota((span, 8, 128), 1)
    for at in range(0, DEVICES, span):
        part = pl.ds(at, span)
        names = recv[part, 2].astype(F32)
        names = jnp.where(place >= 4, names, pltpu.roll(names, 4, 1)).astype(jnp.int32) - 1
        same = names == lane // 4
        for g in range(2):
            chosen = (same & (lane % 4 == 2 * g + place // 4)).astype(F32)
            far += dot(
                chosen.reshape(span * 8, 128).astype(BF16), recv[part, g].reshape(span * 8, 128), TN
            )
    for l in range(LEAVES):
        rows = unfold(far[l * 4 : (l + 1) * 4, :])
        local = (rows + lowered[:, l * RANK : (l + 1) * RANK]).astype(BF16)
        out[l] = near_field[l] + dot(local, target_basis[l])


def final(coarse_list, recv, near_field, target_basis, coarse_couplings, down_transfer):
    vmem = pl.BlockSpec(memory_space=pltpu.VMEM)
    return pl.pallas_call(
        final_kernel,
        out_shape=jax.ShapeDtypeStruct((LEAVES, RHS, POINTS), F32),
        in_specs=[vmem] * 6,
        out_specs=vmem,
        compiler_params=pltpu.CompilerParams(vmem_limit_bytes=24 * MIB),
        name="final",
    )(coarse_list, recv, near_field, target_basis, coarse_couplings, down_transfer)


def body(
    charges,
    near_list,
    near_blocks,
    source_basis,
    target_basis,
    far_devices,
    far_slots,
    far_couplings,
    up_transfer,
    coarse_list,
    coarse_couplings,
    down_transfer,
):
    count = lax.axis_size(AXES)
    of_subtree = lax.axis_size("dev")
    pairs = [[(i, i + 1) for i in range(start, count - 1, 2)] for start in (0, 1)]
    ends = [(i, j) for i, j in pairs[1] if j % of_subtree == 0]
    inner = [(i, j) for i, j in pairs[1] if j % of_subtree != 0]
    first, far_second = [
        lax.ppermute(charges, AXES, some + [(j, i) for i, j in some]) for some in (pairs[0], ends)
    ]
    earlier, mine = lax.optimization_barrier((triangle(), charges))
    send = outgoing(earlier, far_devices, far_slots, mine, source_basis, far_couplings, up_transfer)
    send, mine = lax.optimization_barrier((send, mine))
    recv = lax.all_to_all(send, AXES, 0, 0, tiled=True)
    second = lax.ppermute(mine, AXES, inner + [(j, i) for i, j in inner])
    partial = near_first(mine, first, near_blocks)
    near_field = near_second(near_list, mine, first, second, far_second, near_blocks, partial)
    return final(coarse_list, recv, near_field, target_basis, coarse_couplings, down_transfer)


def solution(mesh):
    return jax.shard_map(
        body,
        mesh=mesh,
        in_specs=(P(AXES),) * 12,
        out_specs=P(AXES),
        check_vma=False,
    )
```

```python
import jax
import jax.numpy as jnp
from jax import lax
from jax.experimental import pallas as pl
from jax.experimental.pallas import tpu as pltpu
from jax.sharding import PartitionSpec as P

AXES = ("grp", "dev")
LEAVES = 32
RHS = 8
RANK = 64
POINTS = 256
NFAR = 8
NNEAR = 4
NCOARSE = 6
DEVICES = 128
BF16 = jnp.bfloat16
F32 = jnp.float32
NT = (((1,), (1,)), ((), ()))
TN = (((0,), (0,)), ((), ()))
MIB = 1 << 20
TRIANGLE_FLOPS = 26843545600
NEAR_FLOPS = 4600000000


def dot(a, b, dims=(((1,), (0,)), ((), ()))):
    return lax.dot_general(a, b, dims, preferred_element_type=F32)


def iota(shape, dim):
    return lax.broadcasted_iota(jnp.int32, shape, dim)


WRITE = 512


def in_hbm(*arrays):
    return tuple(pltpu.with_memory_space_constraint(array, pltpu.HBM) for array in arrays)


def triangle_kernel(earlier):
    earlier[...] = (iota(earlier.shape, 0) < iota(earlier.shape, 1)).astype(BF16)


def triangle():
    entries = LEAVES * NFAR
    return pl.pallas_call(
        triangle_kernel,
        out_shape=jax.ShapeDtypeStruct((entries, entries), BF16),
        out_specs=pl.BlockSpec(memory_space=pltpu.VMEM),
        compiler_params=pltpu.CompilerParams(vmem_limit_bytes=8 * MIB),
        cost_estimate=pl.CostEstimate(flops=TRIANGLE_FLOPS, bytes_accessed=1000, transcendentals=0),
        name="triangle",
    )()


def outgoing_kernel(
    earlier, devices, slots, charges, basis, couplings, transfer, send_hbm, send, products, sems
):
    entries = LEAVES * NFAR
    device = jnp.concatenate([devices[j : j + 1, :] for j in range(NFAR)], axis=1)
    slot = jnp.concatenate([slots[j : j + 1, :] for j in range(NFAR)], axis=1)
    named = iota((DEVICES, entries), 0) == device
    counts = dot(named.astype(BF16), earlier[...])
    order = jnp.sum(jnp.where(named, counts, 0.0), axis=0, keepdims=True).astype(jnp.int32)
    row_of = device * 8 + order
    slot_rows = jnp.broadcast_to((slot + 1).astype(F32), (128, entries)).astype(BF16)

    moments = []
    for at in range(0, LEAVES, 4):
        own = charges[at : at + 4].reshape(4 * RHS, POINTS)
        product = dot(own, basis[at : at + 4].reshape(4 * RANK, POINTS), NT)
        for i in range(4):
            moments.append(product[i * RHS : (i + 1) * RHS, i * RANK : (i + 1) * RANK].astype(BF16))
    raised = []
    for at in range(0, LEAVES, 4):
        product = dot(
            jnp.concatenate(moments[at : at + 4], axis=0),
            transfer[at : at + 4].reshape(4 * RANK, RANK),
            NT,
        )
        raised += [product[i * RHS : (i + 1) * RHS, i * RANK : (i + 1) * RANK] for i in range(4)]
    while len(raised) > 1:
        raised = [a + b for a, b in zip(raised[::2], raised[1::2])]
    node = raised[0]

    wide = jnp.concatenate([node, jnp.zeros((RHS, RANK), F32)], axis=1)
    turned = pltpu.roll(pltpu.roll(wide, RANK, 1), 4, 0)
    upper = iota((RHS, 128), 0) < 4
    node_rows = jnp.where(upper, jnp.where(iota((RHS, 128), 1) < RANK, wide, turned), 0.0)

    span = 256
    for at in range(0, DEVICES * 8, span):
        second = (iota((span, entries), 0) + at == row_of + 4).astype(BF16)
        names = dot(second, slot_rows, NT).reshape(span // 8, 8, 128) + node_rows[None]
        send[at // 8 : (at + span) // 8, 2] = names.astype(BF16)
    writes = [pltpu.make_async_copy(send.at[:, 2], send_hbm.at[:, 2], sems.at[0])]
    writes[0].start()

    for l in range(LEAVES):
        for h in range(2):
            half = couplings[l, h * 4 : h * 4 + 4].reshape(4 * RANK, RANK)
            product = dot(moments[l], half, NT)
            for t in range(2):
                products[2 * h + t, l * RHS : (l + 1) * RHS, :] = product[:, t * 128 : (t + 1) * 128]

    low = iota((LEAVES, 128), 1) < RANK
    pieces = []
    for c in range(4):
        piece = []
        for t in range(NFAR // 2):
            first = products[t, pl.ds(c, LEAVES, stride=RHS), :]
            second = products[t, pl.ds(c + 4, LEAVES, stride=RHS), :]
            piece.append(jnp.where(low, first, pltpu.roll(second, RANK, 1)))
            piece.append(jnp.where(low, pltpu.roll(first, RANK, 1), second))
        pieces.append(jnp.concatenate(piece, axis=0).astype(BF16))
    table = jnp.concatenate(
        [
            jnp.concatenate([pieces[0], pieces[2]], axis=1),
            jnp.concatenate([pieces[1], pieces[3]], axis=1),
        ],
        axis=0,
    )
    for at in range(0, DEVICES * 8, span):
        row = iota((span, entries), 0) + at
        chosen = (row == row_of).astype(BF16)
        second = (row == row_of + 4).astype(BF16)
        rows = dot(jnp.concatenate([chosen, second], axis=1), table)
        part = pl.ds(at // 8, span // 8)
        send[part, 0] = rows[:, :128].reshape(span // 8, 8, 128).astype(BF16)
        send[part, 1] = rows[:, 128:].reshape(span // 8, 8, 128).astype(BF16)
        if (at + span) % WRITE == 0:
            part = pl.ds((at + span - WRITE) // 8, WRITE // 8)
            writes.append(
                pltpu.make_async_copy(send.at[part, 0:2], send_hbm.at[part, 0:2], sems.at[len(writes)])
            )
            writes[-1].start()
    for write in writes:
        write.wait()


def outgoing(earlier, far_devices, far_slots, charges, source_basis, far_couplings, up_transfer):
    vmem = pl.BlockSpec(memory_space=pltpu.VMEM)
    return pl.pallas_call(
        outgoing_kernel,
        out_shape=jax.ShapeDtypeStruct((DEVICES, 3, 8, 128), BF16),
        in_specs=[vmem] * 7,
        out_specs=pl.BlockSpec(memory_space=pltpu.HBM),
        scratch_shapes=[
            pltpu.VMEM((DEVICES, 3, 8, 128), BF16),
            pltpu.VMEM((NFAR // 2, LEAVES * RHS, 128), F32),
            pltpu.SemaphoreType.DMA((1 + DEVICES * 8 // WRITE,)),
        ],
        compiler_params=pltpu.CompilerParams(vmem_limit_bytes=24 * MIB),
        cost_estimate=pl.CostEstimate(flops=26843545600, bytes_accessed=1000, transcendentals=0),
        name="outgoing",
    )(earlier, far_devices.T, far_slots.T, charges, source_basis, far_couplings, up_transfer)


def position():
    return lax.axis_index(AXES)


def near_term(source, blocks, l, j):
    half = POINTS // 2
    return [dot(source, blocks[l, j, at : at + half], NT) for at in (0, half)]


def near_first_kernel(charges, first, blocks, out):
    j = 2 - position() % 2
    half = POINTS // 2
    for l in range(LEAVES):
        own = near_term(charges[l], blocks, l, 0)
        other = near_term(first[l], blocks, l, j)
        out[l, :, :half] = own[0] + other[0]
        out[l, :, half:] = own[1] + other[1]


def near_second_kernel(
    near_list, charges, first, second, far_second, blocks, partial, out, sources, listed, sem
):
    copy = pltpu.make_async_copy(near_list, listed, sem)
    copy.start()
    me = position()
    parity = me % 2
    half = POINTS // 2
    edge = jnp.where(me == 0, charges[0], jnp.where(me == DEVICES - 1, charges[LEAVES - 1], 0.0))
    sources[LEAVES : 2 * LEAVES] = charges[...]
    sources[pl.ds((1 - parity) * 2 * LEAVES, LEAVES)] = first[...]
    for l in range(LEAVES):
        source = second[l] + far_second[l]
        sources[parity * 2 * LEAVES + l] = source
        term = near_term(source + edge, blocks, l, 1 + parity)
        out[l, :, :half] = partial[l, :, :half] + term[0]
        out[l, :, half:] = partial[l, :, half:] + term[1]
    copy.wait()
    base = me * LEAVES - LEAVES
    for l in range(LEAVES):
        term = near_term(sources[listed[NNEAR - 1, l] - base], blocks, l, NNEAR - 1)
        out[l, :, :half] += term[0]
        out[l, :, half:] += term[1]


def near(kernel, name, arrays, scratch_shapes=()):
    return pl.pallas_call(
        kernel,
        out_shape=jax.ShapeDtypeStruct((LEAVES, RHS, POINTS), F32),
        in_specs=[pl.BlockSpec(memory_space=pltpu.VMEM)] * len(arrays),
        out_specs=pl.BlockSpec(memory_space=pltpu.VMEM),
        scratch_shapes=scratch_shapes,
        compiler_params=pltpu.CompilerParams(vmem_limit_bytes=20 * MIB),
        cost_estimate=pl.CostEstimate(flops=NEAR_FLOPS, bytes_accessed=1000, transcendentals=0),
        name=name,
    )(*arrays)


def near_first(charges, first, near_blocks):
    return near(near_first_kernel, "near_first", (charges, first, near_blocks))


def near_second(near_list, charges, first, second, far_second, near_blocks, partial):
    return near(
        near_second_kernel,
        "near_second",
        (near_list.T, charges, first, second, far_second, near_blocks, partial),
        (
            pltpu.VMEM((3 * LEAVES, RHS, POINTS), BF16),
            pltpu.SMEM((NNEAR, LEAVES), jnp.int32),
            pltpu.SemaphoreType.DMA,
        ),
    )


def unfold(rows):
    return jnp.concatenate([rows[:, :RANK], rows[:, RANK:]], axis=0)


def final_kernel(coarse_list, recv, near_field, target_basis, couplings, transfer, out):
    shape = (NCOARSE * 4, NCOARSE)
    listed = jnp.where(iota(shape, 0) // 4 == iota(shape, 1), coarse_list[...], 0)
    row_of = jnp.sum(listed, axis=1, keepdims=True) * 8 + iota((NCOARSE * 4, 1), 0) % 4
    node = (iota((NCOARSE * 4, DEVICES * 8), 1) == row_of).astype(BF16)

    span = 32
    lane = iota((span, 8, 128), 2)
    place = iota((span, 8, 128), 1)
    piece = [lane % 4 == 2 * g + place // 4 for g in range(2)]
    slot = (lane // 4 + 1).astype(F32)

    def far_part(at):
        part = pl.ds(at, span)
        names = recv[part, 2].astype(F32)
        same = jnp.where(place >= 4, names, pltpu.roll(names, 4, 1)) == slot
        terms = [
            dot(
                jnp.where(same & piece[g], 1.0, 0.0).reshape(span * 8, 128).astype(BF16),
                recv[part, g].reshape(span * 8, 128),
                TN,
            )
            for g in range(2)
        ]
        return terms[0] + terms[1]

    picked = dot(node, recv[:, 2].reshape(DEVICES * 8, 128)).astype(BF16)
    far = far_part(0)
    coarse = [dot(unfold(picked[4 * j : 4 * j + 4]), couplings[0, j], NT) for j in range(NCOARSE)]
    far += far_part(span)
    coarse = ((coarse[0] + coarse[1]) + (coarse[2] + coarse[3])) + (coarse[4] + coarse[5])
    far += far_part(2 * span)
    lowered = dot(coarse.astype(BF16), transfer[...].reshape(LEAVES * RANK, RANK), NT)
    far += far_part(3 * span)
    upper = iota((RHS, 128), 0) < 4
    for l in range(0, LEAVES, 2):
        rows = far[l * 4 : l * 4 + 8, :]
        swapped = pltpu.roll(rows, RANK, 1)
        turned = pltpu.roll(rows, 4, 0)
        pair = lowered[:, l * RANK : (l + 2) * RANK]
        even = jnp.where(upper, rows, pltpu.roll(swapped, 4, 0)) + pair
        odd = jnp.where(upper, turned, swapped) + pltpu.roll(pair, RANK, 1)
        for i, local in enumerate((even, odd)):
            out[l + i] = near_field[l + i] + dot(local[:, :RANK].astype(BF16), target_basis[l + i])


def final(coarse_list, recv, near_field, target_basis, coarse_couplings, down_transfer):
    vmem = pl.BlockSpec(memory_space=pltpu.VMEM)
    return pl.pallas_call(
        final_kernel,
        out_shape=jax.ShapeDtypeStruct((LEAVES, RHS, POINTS), F32),
        in_specs=[vmem] * 6,
        out_specs=vmem,
        compiler_params=pltpu.CompilerParams(vmem_limit_bytes=24 * MIB),
        name="final",
    )(coarse_list, recv, near_field, target_basis, coarse_couplings, down_transfer)


def body(
    charges,
    near_list,
    near_blocks,
    source_basis,
    target_basis,
    far_devices,
    far_slots,
    far_couplings,
    up_transfer,
    coarse_list,
    coarse_couplings,
    down_transfer,
):
    count = lax.axis_size(AXES)
    of_subtree = lax.axis_size("dev")
    pairs = [[(i, i + 1) for i in range(start, count - 1, 2)] for start in (0, 1)]
    ends = [(i, j) for i, j in pairs[1] if j % of_subtree == 0]
    inner = [(i, j) for i, j in pairs[1] if j % of_subtree != 0]
    first, far_second = [
        lax.ppermute(charges, AXES, some + [(j, i) for i, j in some]) for some in (pairs[0], ends)
    ]
    earlier, mine = lax.optimization_barrier((triangle(), charges))
    send = outgoing(earlier, far_devices, far_slots, mine, source_basis, far_couplings, up_transfer)
    send, mine = lax.optimization_barrier((send, mine))
    recv = lax.all_to_all(send, AXES, 0, 0, tiled=True)
    second = lax.ppermute(mine, AXES, inner + [(j, i) for i, j in inner])
    partial = near_first(mine, first, near_blocks)
    near_field = near_second(near_list, mine, first, second, far_second, near_blocks, partial)
    return final(coarse_list, recv, near_field, target_basis, coarse_couplings, down_transfer)


def solution(mesh):
    return jax.shard_map(
        body,
        mesh=mesh,
        in_specs=(P(AXES),) * 12,
        out_specs=P(AXES),
        check_vma=False,
    )
```

```python
import jax
import jax.numpy as jnp
from jax import lax
from jax.experimental import pallas as pl
from jax.experimental.pallas import tpu as pltpu
from jax.sharding import PartitionSpec as P

AXES = ("grp", "dev")
LEAVES = 32
RHS = 8
RANK = 64
POINTS = 256
NFAR = 8
NNEAR = 4
NCOARSE = 6
DEVICES = 128
BF16 = jnp.bfloat16
F32 = jnp.float32
NT = (((1,), (1,)), ((), ()))
TN = (((0,), (0,)), ((), ()))
MIB = 1 << 20
TRIANGLE_FLOPS = 26843545600
NEAR_FLOPS = 4600000000


def dot(a, b, dims=(((1,), (0,)), ((), ()))):
    return lax.dot_general(a, b, dims, preferred_element_type=F32)


def iota(shape, dim):
    return lax.broadcasted_iota(jnp.int32, shape, dim)


WRITE = 512


def in_hbm(*arrays):
    return tuple(pltpu.with_memory_space_constraint(array, pltpu.HBM) for array in arrays)


def triangle_kernel(earlier):
    earlier[...] = (iota(earlier.shape, 0) < iota(earlier.shape, 1)).astype(BF16)


def triangle():
    entries = LEAVES * NFAR
    return pl.pallas_call(
        triangle_kernel,
        out_shape=jax.ShapeDtypeStruct((entries, entries), BF16),
        out_specs=pl.BlockSpec(memory_space=pltpu.VMEM),
        compiler_params=pltpu.CompilerParams(vmem_limit_bytes=8 * MIB),
        cost_estimate=pl.CostEstimate(flops=TRIANGLE_FLOPS, bytes_accessed=1000, transcendentals=0),
        name="triangle",
    )()


def outgoing_kernel(
    earlier, devices, slots, charges, basis, couplings, transfer, send_hbm, send, products, sems
):
    entries = LEAVES * NFAR
    device = jnp.concatenate([devices[j : j + 1, :] for j in range(NFAR)], axis=1)
    slot = jnp.concatenate([slots[j : j + 1, :] for j in range(NFAR)], axis=1)
    named = iota((DEVICES, entries), 0) == device
    counts = dot(named.astype(BF16), earlier[...])
    order = jnp.sum(jnp.where(named, counts, 0.0), axis=0, keepdims=True).astype(jnp.int32)
    row_of = device * 8 + order
    slot_rows = jnp.broadcast_to((slot + 1).astype(F32), (128, entries)).astype(BF16)

    moments = []
    for at in range(0, LEAVES, 4):
        own = charges[at : at + 4].reshape(4 * RHS, POINTS)
        product = dot(own, basis[at : at + 4].reshape(4 * RANK, POINTS), NT)
        for i in range(4):
            moments.append(product[i * RHS : (i + 1) * RHS, i * RANK : (i + 1) * RANK].astype(BF16))
    raised = []
    for at in range(0, LEAVES, 4):
        product = dot(
            jnp.concatenate(moments[at : at + 4], axis=0),
            transfer[at : at + 4].reshape(4 * RANK, RANK),
            NT,
        )
        raised += [product[i * RHS : (i + 1) * RHS, i * RANK : (i + 1) * RANK] for i in range(4)]
    while len(raised) > 1:
        raised = [a + b for a, b in zip(raised[::2], raised[1::2])]
    node = raised[0]

    wide = jnp.concatenate([node, jnp.zeros((RHS, RANK), F32)], axis=1)
    turned = pltpu.roll(pltpu.roll(wide, RANK, 1), 4, 0)
    upper = iota((RHS, 128), 0) < 4
    node_rows = jnp.where(upper, jnp.where(iota((RHS, 128), 1) < RANK, wide, turned), 0.0)

    span = 256
    for at in range(0, DEVICES * 8, span):
        second = (iota((span, entries), 0) + at == row_of + 4).astype(BF16)
        names = dot(second, slot_rows, NT).reshape(span // 8, 8, 128) + node_rows[None]
        send[at // 8 : (at + span) // 8, 2] = names.astype(BF16)
    writes = [pltpu.make_async_copy(send.at[:, 2], send_hbm.at[:, 2], sems.at[0])]
    writes[0].start()

    shape = (2 * RHS, 128)
    own_half = (iota(shape, 0) < RHS) == (iota(shape, 1) < RANK)
    for l in range(0, LEAVES, 2):
        both = jnp.concatenate(moments[l : l + 2], axis=0).astype(F32)
        both = jnp.where(own_half, jnp.concatenate([both, both], axis=1), 0.0).astype(BF16)
        for h in range(2):
            pair = [couplings[l + i, h * 4 : h * 4 + 4].reshape(4 * RANK, RANK) for i in range(2)]
            product = dot(both, jnp.concatenate(pair, axis=1), NT)
            for t in range(2):
                products[2 * h + t, l * RHS : (l + 2) * RHS, :] = product[:, t * 128 : (t + 1) * 128]

    low = iota((LEAVES, 128), 1) < RANK
    pieces = []
    for c in range(4):
        piece = []
        for t in range(NFAR // 2):
            first = products[t, pl.ds(c, LEAVES, stride=RHS), :]
            second = products[t, pl.ds(c + 4, LEAVES, stride=RHS), :]
            piece.append(jnp.where(low, first, pltpu.roll(second, RANK, 1)))
            piece.append(jnp.where(low, pltpu.roll(first, RANK, 1), second))
        pieces.append(jnp.concatenate(piece, axis=0).astype(BF16))
    table = jnp.concatenate(
        [
            jnp.concatenate([pieces[0], pieces[2]], axis=1),
            jnp.concatenate([pieces[1], pieces[3]], axis=1),
        ],
        axis=0,
    )
    for at in range(0, DEVICES * 8, span):
        row = iota((span, entries), 0) + at
        chosen = (row == row_of).astype(BF16)
        second = (row == row_of + 4).astype(BF16)
        rows = dot(jnp.concatenate([chosen, second], axis=1), table)
        part = pl.ds(at // 8, span // 8)
        send[part, 0] = rows[:, :128].reshape(span // 8, 8, 128).astype(BF16)
        send[part, 1] = rows[:, 128:].reshape(span // 8, 8, 128).astype(BF16)
        if (at + span) % WRITE == 0:
            part = pl.ds((at + span - WRITE) // 8, WRITE // 8)
            writes.append(
                pltpu.make_async_copy(send.at[part, 0:2], send_hbm.at[part, 0:2], sems.at[len(writes)])
            )
            writes[-1].start()
    for write in writes:
        write.wait()


def outgoing(earlier, far_devices, far_slots, charges, source_basis, far_couplings, up_transfer):
    vmem = pl.BlockSpec(memory_space=pltpu.VMEM)
    return pl.pallas_call(
        outgoing_kernel,
        out_shape=jax.ShapeDtypeStruct((DEVICES, 3, 8, 128), BF16),
        in_specs=[vmem] * 7,
        out_specs=pl.BlockSpec(memory_space=pltpu.HBM),
        scratch_shapes=[
            pltpu.VMEM((DEVICES, 3, 8, 128), BF16),
            pltpu.VMEM((NFAR // 2, LEAVES * RHS, 128), F32),
            pltpu.SemaphoreType.DMA((1 + DEVICES * 8 // WRITE,)),
        ],
        compiler_params=pltpu.CompilerParams(vmem_limit_bytes=24 * MIB),
        cost_estimate=pl.CostEstimate(flops=26843545600, bytes_accessed=1000, transcendentals=0),
        name="outgoing",
    )(earlier, far_devices.T, far_slots.T, charges, source_basis, far_couplings, up_transfer)


def position():
    return lax.axis_index(AXES)


def near_term(source, blocks, l, j):
    half = POINTS // 2
    return [dot(source, blocks[l, j, at : at + half], NT) for at in (0, half)]


def near_first_kernel(charges, first, blocks, out):
    j = 2 - position() % 2
    half = POINTS // 2
    for l in range(LEAVES):
        own = near_term(charges[l], blocks, l, 0)
        other = near_term(first[l], blocks, l, j)
        out[l, :, :half] = own[0] + other[0]
        out[l, :, half:] = own[1] + other[1]


def near_second_kernel(
    near_list, charges, first, second, far_second, blocks, partial, out, sources, listed, sem
):
    copy = pltpu.make_async_copy(near_list, listed, sem)
    copy.start()
    me = position()
    parity = me % 2
    half = POINTS // 2
    edge = jnp.where(me == 0, charges[0], jnp.where(me == DEVICES - 1, charges[LEAVES - 1], 0.0))
    sources[LEAVES : 2 * LEAVES] = charges[...]
    sources[pl.ds((1 - parity) * 2 * LEAVES, LEAVES)] = first[...]
    for l in range(LEAVES):
        source = second[l] + far_second[l]
        sources[parity * 2 * LEAVES + l] = source
        term = near_term(source + edge, blocks, l, 1 + parity)
        out[l, :, :half] = partial[l, :, :half] + term[0]
        out[l, :, half:] = partial[l, :, half:] + term[1]
    copy.wait()
    base = me * LEAVES - LEAVES
    for l in range(LEAVES):
        term = near_term(sources[listed[NNEAR - 1, l] - base], blocks, l, NNEAR - 1)
        out[l, :, :half] += term[0]
        out[l, :, half:] += term[1]


def near(kernel, name, arrays, scratch_shapes=()):
    return pl.pallas_call(
        kernel,
        out_shape=jax.ShapeDtypeStruct((LEAVES, RHS, POINTS), F32),
        in_specs=[pl.BlockSpec(memory_space=pltpu.VMEM)] * len(arrays),
        out_specs=pl.BlockSpec(memory_space=pltpu.VMEM),
        scratch_shapes=scratch_shapes,
        compiler_params=pltpu.CompilerParams(vmem_limit_bytes=20 * MIB),
        cost_estimate=pl.CostEstimate(flops=NEAR_FLOPS, bytes_accessed=1000, transcendentals=0),
        name=name,
    )(*arrays)


def near_first(charges, first, near_blocks):
    return near(near_first_kernel, "near_first", (charges, first, near_blocks))


def near_second(near_list, charges, first, second, far_second, near_blocks, partial):
    return near(
        near_second_kernel,
        "near_second",
        (near_list.T, charges, first, second, far_second, near_blocks, partial),
        (
            pltpu.VMEM((3 * LEAVES, RHS, POINTS), BF16),
            pltpu.SMEM((NNEAR, LEAVES), jnp.int32),
            pltpu.SemaphoreType.DMA,
        ),
    )


def unfold(rows):
    return jnp.concatenate([rows[:, :RANK], rows[:, RANK:]], axis=0)


def final_kernel(coarse_list, recv, near_field, target_basis, couplings, transfer, out):
    shape = (NCOARSE * 4, NCOARSE)
    listed = jnp.where(iota(shape, 0) // 4 == iota(shape, 1), coarse_list[...], 0)
    row_of = jnp.sum(listed, axis=1, keepdims=True) * 8 + iota((NCOARSE * 4, 1), 0) % 4
    node = (iota((NCOARSE * 4, DEVICES * 8), 1) == row_of).astype(BF16)

    span = 32
    lane = iota((span, 8, 128), 2)
    place = iota((span, 8, 128), 1)
    piece = [lane % 4 == 2 * g + place // 4 for g in range(2)]
    slot = (lane // 4 + 1).astype(F32)

    def far_part(at):
        part = pl.ds(at, span)
        names = recv[part, 2].astype(F32)
        same = jnp.where(place >= 4, names, pltpu.roll(names, 4, 1)) == slot
        terms = [
            dot(
                jnp.where(same & piece[g], 1.0, 0.0).reshape(span * 8, 128).astype(BF16),
                recv[part, g].reshape(span * 8, 128),
                TN,
            )
            for g in range(2)
        ]
        return terms[0] + terms[1]

    picked = dot(node, recv[:, 2].reshape(DEVICES * 8, 128)).astype(BF16)
    far = (far_part(0) + far_part(span)) + (far_part(2 * span) + far_part(3 * span))
    coarse = [dot(unfold(picked[4 * j : 4 * j + 4]), couplings[0, j], NT) for j in range(NCOARSE)]
    coarse = ((coarse[0] + coarse[1]) + (coarse[2] + coarse[3])) + (coarse[4] + coarse[5])
    lowered = dot(coarse.astype(BF16), transfer[...].reshape(LEAVES * RANK, RANK), NT)
    upper = iota((RHS, 128), 0) < 4
    for l in range(0, LEAVES, 2):
        rows = far[l * 4 : l * 4 + 8, :]
        swapped = pltpu.roll(rows, RANK, 1)
        turned = pltpu.roll(rows, 4, 0)
        pair = lowered[:, l * RANK : (l + 2) * RANK]
        even = jnp.where(upper, rows, pltpu.roll(swapped, 4, 0)) + pair
        odd = jnp.where(upper, turned, swapped) + pltpu.roll(pair, RANK, 1)
        for i, local in enumerate((even, odd)):
            out[l + i] = near_field[l + i] + dot(local[:, :RANK].astype(BF16), target_basis[l + i])


def final(coarse_list, recv, near_field, target_basis, coarse_couplings, down_transfer):
    vmem = pl.BlockSpec(memory_space=pltpu.VMEM)
    return pl.pallas_call(
        final_kernel,
        out_shape=jax.ShapeDtypeStruct((LEAVES, RHS, POINTS), F32),
        in_specs=[vmem] * 6,
        out_specs=vmem,
        compiler_params=pltpu.CompilerParams(vmem_limit_bytes=24 * MIB),
        name="final",
    )(coarse_list, recv, near_field, target_basis, coarse_couplings, down_transfer)


def body(
    charges,
    near_list,
    near_blocks,
    source_basis,
    target_basis,
    far_devices,
    far_slots,
    far_couplings,
    up_transfer,
    coarse_list,
    coarse_couplings,
    down_transfer,
):
    count = lax.axis_size(AXES)
    of_subtree = lax.axis_size("dev")
    pairs = [[(i, i + 1) for i in range(start, count - 1, 2)] for start in (0, 1)]
    ends = [(i, j) for i, j in pairs[1] if j % of_subtree == 0]
    inner = [(i, j) for i, j in pairs[1] if j % of_subtree != 0]
    first, far_second = [
        lax.ppermute(charges, AXES, some + [(j, i) for i, j in some]) for some in (pairs[0], ends)
    ]
    earlier, mine = lax.optimization_barrier((triangle(), charges))
    send = outgoing(earlier, far_devices, far_slots, mine, source_basis, far_couplings, up_transfer)
    send, mine = lax.optimization_barrier((send, mine))
    recv = lax.all_to_all(send, AXES, 0, 0, tiled=True)
    second = lax.ppermute(mine, AXES, inner + [(j, i) for i, j in inner])
    partial = near_first(mine, first, near_blocks)
    near_field = near_second(near_list, mine, first, second, far_second, near_blocks, partial)
    return final(coarse_list, recv, near_field, target_basis, coarse_couplings, down_transfer)


def solution(mesh):
    return jax.shard_map(
        body,
        mesh=mesh,
        in_specs=(P(AXES),) * 12,
        out_specs=P(AXES),
        check_vma=False,
    )
```

```python
import jax
import jax.numpy as jnp
from jax import lax
from jax.experimental import pallas as pl
from jax.experimental.pallas import tpu as pltpu
from jax.sharding import PartitionSpec as P

AXES = ("grp", "dev")
LEAVES = 32
RHS = 8
RANK = 64
POINTS = 256
NFAR = 8
NNEAR = 4
NCOARSE = 6
DEVICES = 128
BF16 = jnp.bfloat16
F32 = jnp.float32
NT = (((1,), (1,)), ((), ()))
TN = (((0,), (0,)), ((), ()))
MIB = 1 << 20
TRIANGLE_FLOPS = 26843545600
NEAR_FLOPS = 4600000000


def dot(a, b, dims=(((1,), (0,)), ((), ()))):
    return lax.dot_general(a, b, dims, preferred_element_type=F32)


def iota(shape, dim):
    return lax.broadcasted_iota(jnp.int32, shape, dim)


WRITE = 512


def in_hbm(*arrays):
    return tuple(pltpu.with_memory_space_constraint(array, pltpu.HBM) for array in arrays)


def triangle_kernel(earlier):
    earlier[...] = (iota(earlier.shape, 0) < iota(earlier.shape, 1)).astype(BF16)


def triangle():
    entries = LEAVES * NFAR
    return pl.pallas_call(
        triangle_kernel,
        out_shape=jax.ShapeDtypeStruct((entries, entries), BF16),
        out_specs=pl.BlockSpec(memory_space=pltpu.VMEM),
        compiler_params=pltpu.CompilerParams(vmem_limit_bytes=8 * MIB),
        cost_estimate=pl.CostEstimate(flops=TRIANGLE_FLOPS, bytes_accessed=1000, transcendentals=0),
        name="triangle",
    )()


def outgoing_kernel(
    earlier, devices, slots, charges, basis, couplings, transfer, send_hbm, send, products, sems
):
    entries = LEAVES * NFAR
    device = jnp.concatenate([devices[j : j + 1, :] for j in range(NFAR)], axis=1)
    slot = jnp.concatenate([slots[j : j + 1, :] for j in range(NFAR)], axis=1)
    named = iota((DEVICES, entries), 0) == device
    counts = dot(named.astype(BF16), earlier[...])
    order = jnp.sum(jnp.where(named, counts, 0.0), axis=0, keepdims=True).astype(jnp.int32)
    row_of = device * 8 + order
    slot_rows = jnp.broadcast_to((slot + 1).astype(F32), (128, entries)).astype(BF16)

    moments = []
    for at in range(0, LEAVES, 4):
        own = charges[at : at + 4].reshape(4 * RHS, POINTS)
        product = dot(own, basis[at : at + 4].reshape(4 * RANK, POINTS), NT)
        for i in range(4):
            moments.append(product[i * RHS : (i + 1) * RHS, i * RANK : (i + 1) * RANK].astype(BF16))
    raised = []
    for at in range(0, LEAVES, 4):
        product = dot(
            jnp.concatenate(moments[at : at + 4], axis=0),
            transfer[at : at + 4].reshape(4 * RANK, RANK),
            NT,
        )
        raised += [product[i * RHS : (i + 1) * RHS, i * RANK : (i + 1) * RANK] for i in range(4)]
    while len(raised) > 1:
        raised = [a + b for a, b in zip(raised[::2], raised[1::2])]
    node = raised[0]

    wide = jnp.concatenate([node, jnp.zeros((RHS, RANK), F32)], axis=1)
    turned = pltpu.roll(pltpu.roll(wide, RANK, 1), 4, 0)
    upper = iota((RHS, 128), 0) < 4
    node_rows = jnp.where(upper, jnp.where(iota((RHS, 128), 1) < RANK, wide, turned), 0.0)

    span = 256
    for at in range(0, DEVICES * 8, span):
        second = (iota((span, entries), 0) + at == row_of + 4).astype(BF16)
        names = dot(second, slot_rows, NT).reshape(span // 8, 8, 128) + node_rows[None]
        send[at // 8 : (at + span) // 8, 2] = names.astype(BF16)
    writes = [pltpu.make_async_copy(send.at[:, 2], send_hbm.at[:, 2], sems.at[0])]
    writes[0].start()

    shape = (2 * RHS, 128)
    own_half = (iota(shape, 0) < RHS) == (iota(shape, 1) < RANK)
    for l in range(0, LEAVES, 2):
        both = jnp.concatenate(moments[l : l + 2], axis=0).astype(F32)
        both = jnp.where(own_half, jnp.concatenate([both, both], axis=1), 0.0).astype(BF16)
        for h in range(2):
            pair = [couplings[l + i, h * 4 : h * 4 + 4].reshape(4 * RANK, RANK) for i in range(2)]
            product = dot(both, jnp.concatenate(pair, axis=1), NT)
            for t in range(2):
                products[2 * h + t, l * RHS : (l + 2) * RHS, :] = product[:, t * 128 : (t + 1) * 128]

    low = iota((LEAVES, 128), 1) < RANK
    pieces = []
    for c in range(4):
        piece = []
        for t in range(NFAR // 2):
            first = products[t, pl.ds(c, LEAVES, stride=RHS), :]
            second = products[t, pl.ds(c + 4, LEAVES, stride=RHS), :]
            piece.append(jnp.where(low, first, pltpu.roll(second, RANK, 1)))
            piece.append(jnp.where(low, pltpu.roll(first, RANK, 1), second))
        pieces.append(jnp.concatenate(piece, axis=0).astype(BF16))
    table = jnp.concatenate(
        [
            jnp.concatenate([pieces[0], pieces[2]], axis=1),
            jnp.concatenate([pieces[1], pieces[3]], axis=1),
        ],
        axis=0,
    )
    for at in range(0, DEVICES * 8, span):
        row = iota((span, entries), 0) + at
        chosen = (row == row_of).astype(BF16)
        second = (row == row_of + 4).astype(BF16)
        rows = dot(jnp.concatenate([chosen, second], axis=1), table)
        part = pl.ds(at // 8, span // 8)
        send[part, 0] = rows[:, :128].reshape(span // 8, 8, 128).astype(BF16)
        send[part, 1] = rows[:, 128:].reshape(span // 8, 8, 128).astype(BF16)
        if (at + span) % WRITE == 0:
            part = pl.ds((at + span - WRITE) // 8, WRITE // 8)
            writes.append(
                pltpu.make_async_copy(send.at[part, 0:2], send_hbm.at[part, 0:2], sems.at[len(writes)])
            )
            writes[-1].start()
    for write in writes:
        write.wait()


def outgoing(earlier, far_devices, far_slots, charges, source_basis, far_couplings, up_transfer):
    vmem = pl.BlockSpec(memory_space=pltpu.VMEM)
    return pl.pallas_call(
        outgoing_kernel,
        out_shape=jax.ShapeDtypeStruct((DEVICES, 3, 8, 128), BF16),
        in_specs=[vmem] * 7,
        out_specs=pl.BlockSpec(memory_space=pltpu.HBM),
        scratch_shapes=[
            pltpu.VMEM((DEVICES, 3, 8, 128), BF16),
            pltpu.VMEM((NFAR // 2, LEAVES * RHS, 128), F32),
            pltpu.SemaphoreType.DMA((1 + DEVICES * 8 // WRITE,)),
        ],
        compiler_params=pltpu.CompilerParams(vmem_limit_bytes=24 * MIB),
        cost_estimate=pl.CostEstimate(flops=26843545600, bytes_accessed=1000, transcendentals=0),
        name="outgoing",
    )(earlier, far_devices.T, far_slots.T, charges, source_basis, far_couplings, up_transfer)


def position():
    return lax.axis_index(AXES)


def near_term(source, blocks, l, j):
    half = POINTS // 2
    return [dot(source, blocks[l, j, at : at + half], NT) for at in (0, half)]


def near_first_kernel(charges, first, blocks, out):
    j = 2 - position() % 2
    half = POINTS // 2
    for l in range(LEAVES):
        own = near_term(charges[l], blocks, l, 0)
        other = near_term(first[l], blocks, l, j)
        out[l, :, :half] = own[0] + other[0]
        out[l, :, half:] = own[1] + other[1]


def near_second_kernel(
    near_list, charges, first, second, far_second, blocks, partial, out, sources, listed, sem
):
    copy = pltpu.make_async_copy(near_list, listed, sem)
    copy.start()
    me = position()
    parity = me % 2
    half = POINTS // 2
    edge = jnp.where(me == 0, charges[0], jnp.where(me == DEVICES - 1, charges[LEAVES - 1], 0.0))
    sources[LEAVES : 2 * LEAVES] = charges[...]
    sources[pl.ds((1 - parity) * 2 * LEAVES, LEAVES)] = first[...]
    for l in range(LEAVES):
        source = second[l] + far_second[l]
        sources[parity * 2 * LEAVES + l] = source
        term = near_term(source + edge, blocks, l, 1 + parity)
        out[l, :, :half] = partial[l, :, :half] + term[0]
        out[l, :, half:] = partial[l, :, half:] + term[1]
    copy.wait()
    base = me * LEAVES - LEAVES
    for l in range(LEAVES):
        term = near_term(sources[listed[NNEAR - 1, l] - base], blocks, l, NNEAR - 1)
        out[l, :, :half] += term[0]
        out[l, :, half:] += term[1]


def near(kernel, name, arrays, scratch_shapes=()):
    return pl.pallas_call(
        kernel,
        out_shape=jax.ShapeDtypeStruct((LEAVES, RHS, POINTS), F32),
        in_specs=[pl.BlockSpec(memory_space=pltpu.VMEM)] * len(arrays),
        out_specs=pl.BlockSpec(memory_space=pltpu.VMEM),
        scratch_shapes=scratch_shapes,
        compiler_params=pltpu.CompilerParams(vmem_limit_bytes=20 * MIB),
        cost_estimate=pl.CostEstimate(flops=NEAR_FLOPS, bytes_accessed=1000, transcendentals=0),
        name=name,
    )(*arrays)


def near_first(charges, first, near_blocks):
    return near(near_first_kernel, "near_first", (charges, first, near_blocks))


def near_second(near_list, charges, first, second, far_second, near_blocks, partial):
    return near(
        near_second_kernel,
        "near_second",
        (near_list.T, charges, first, second, far_second, near_blocks, partial),
        (
            pltpu.VMEM((3 * LEAVES, RHS, POINTS), BF16),
            pltpu.SMEM((NNEAR, LEAVES), jnp.int32),
            pltpu.SemaphoreType.DMA,
        ),
    )


def unfold(rows):
    return jnp.concatenate([rows[:, :RANK], rows[:, RANK:]], axis=0)


def final_kernel(coarse_list, recv, near_field, target_basis, couplings, transfer, out):
    shape = (NCOARSE * 4, NCOARSE)
    listed = jnp.where(iota(shape, 0) // 4 == iota(shape, 1), coarse_list[...], 0)
    row_of = jnp.sum(listed, axis=1, keepdims=True) * 8 + iota((NCOARSE * 4, 1), 0) % 4
    node = (iota((NCOARSE * 4, DEVICES * 8), 1) == row_of).astype(BF16)

    span = 32
    lane = iota((span, 8, 128), 2)
    place = iota((span, 8, 128), 1)
    piece = [lane % 4 == 2 * g + place // 4 for g in range(2)]
    slot = (lane // 4 + 1).astype(F32)

    def far_part(at):
        part = pl.ds(at, span)
        names = recv[part, 2].astype(F32)
        same = jnp.where(place >= 4, names, pltpu.roll(names, 4, 1)) == slot
        terms = [
            dot(
                jnp.where(same & piece[g], 1.0, 0.0).reshape(span * 8, 128).astype(BF16),
                recv[part, g].reshape(span * 8, 128),
                TN,
            )
            for g in range(2)
        ]
        return terms[0] + terms[1]

    picked = dot(node, recv[:, 2].reshape(DEVICES * 8, 128)).astype(BF16)
    far = (far_part(0) + far_part(span)) + (far_part(2 * span) + far_part(3 * span))
    coarse = [dot(unfold(picked[4 * j : 4 * j + 4]), couplings[0, j], NT) for j in range(NCOARSE)]
    coarse = ((coarse[0] + coarse[1]) + (coarse[2] + coarse[3])) + (coarse[4] + coarse[5])
    lowered = dot(coarse.astype(BF16), transfer[...].reshape(LEAVES * RANK, RANK), NT)
    upper = iota((RHS, 128), 0) < 4
    low = iota((RHS, 128), 1) < RANK
    for l in range(0, LEAVES, 2):
        rows = far[l * 4 : l * 4 + 8, :]
        turned = pltpu.roll(pltpu.roll(rows, RANK, 1), 4, 0)
        pair = lowered[:, l * RANK : (l + 2) * RANK]
        even = jnp.where(low, jnp.where(upper, rows, turned) + pair, 0.0)
        odd = jnp.where(low, 0.0, jnp.where(upper, turned, rows) + pair)
        local = jnp.concatenate([even, odd], axis=0).astype(BF16)
        product = dot(local, target_basis[l : l + 2].reshape(2 * RANK, POINTS))
        out[l] = near_field[l] + product[:RHS]
        out[l + 1] = near_field[l + 1] + product[RHS:]


def final(coarse_list, recv, near_field, target_basis, coarse_couplings, down_transfer):
    vmem = pl.BlockSpec(memory_space=pltpu.VMEM)
    return pl.pallas_call(
        final_kernel,
        out_shape=jax.ShapeDtypeStruct((LEAVES, RHS, POINTS), F32),
        in_specs=[vmem] * 6,
        out_specs=vmem,
        compiler_params=pltpu.CompilerParams(vmem_limit_bytes=24 * MIB),
        name="final",
    )(coarse_list, recv, near_field, target_basis, coarse_couplings, down_transfer)


def body(
    charges,
    near_list,
    near_blocks,
    source_basis,
    target_basis,
    far_devices,
    far_slots,
    far_couplings,
    up_transfer,
    coarse_list,
    coarse_couplings,
    down_transfer,
):
    count = lax.axis_size(AXES)
    of_subtree = lax.axis_size("dev")
    pairs = [[(i, i + 1) for i in range(start, count - 1, 2)] for start in (0, 1)]
    ends = [(i, j) for i, j in pairs[1] if j % of_subtree == 0]
    inner = [(i, j) for i, j in pairs[1] if j % of_subtree != 0]
    first, far_second = [
        lax.ppermute(charges, AXES, some + [(j, i) for i, j in some]) for some in (pairs[0], ends)
    ]
    earlier, mine = lax.optimization_barrier((triangle(), charges))
    send = outgoing(earlier, far_devices, far_slots, mine, source_basis, far_couplings, up_transfer)
    send, mine = lax.optimization_barrier((send, mine))
    recv = lax.all_to_all(send, AXES, 0, 0, tiled=True)
    second = lax.ppermute(mine, AXES, inner + [(j, i) for i, j in inner])
    partial = near_first(mine, first, near_blocks)
    near_field = near_second(near_list, mine, first, second, far_second, near_blocks, partial)
    return final(coarse_list, recv, near_field, target_basis, coarse_couplings, down_transfer)


def solution(mesh):
    return jax.shard_map(
        body,
        mesh=mesh,
        in_specs=(P(AXES),) * 12,
        out_specs=P(AXES),
        check_vma=False,
    )
```
